256 devices in a mesh: rep: 16 (over z_lo, x), exp: 16 (over y, z_hi, core).
Axes of the slice: x: 4, y: 4, z: 8 (z_hi: 2, z_lo: 4; z = z_hi * 4 + z_lo), core: 2. Of those that a mesh axis runs over, the one named last changes fastest.
Arguments:
- w_in: bfloat16 [16, 768, 1536], P('exp'), may hold values from -0.21875 to 0.21875
- w_out: bfloat16 [16, 1536, 768], P('exp'), may hold values from -0.15625 to 0.15625
- mom_in: float32 [16, 768, 1536], P('exp', 'rep'), may hold values from -0.024 to 0.024
- mom_out: float32 [16, 1536, 768], P('exp', 'rep'), may hold values from -0.024 to 0.024
- frames: bfloat16 [16, 2, 2048, 768], P('rep', None, 'exp'), may hold values from -6 to 6
- targets: bfloat16 [16, 2, 2048, 768], P('rep', None, 'exp'), may hold values from -6 to 6
- routes: int32 [16, 2, 2048, 2], P('rep', None, 'exp'), may hold values from 0 to 15, all different within a row; in each aligned block of 128 rows (0 to 127, 128 to 255, ..., all dimensions but the last counted through in order) at most 32 rows name the same one
- gates: float32 [16, 2, 2048, 2], P('rep', None, 'exp'), may hold values from 0.1 to 0.9
Outputs:
- new_w_in: bfloat16 [16, 768, 1536], P('exp')
- new_w_out: bfloat16 [16, 1536, 768], P('exp')
- new_mom_in: float32 [16, 768, 1536], P('exp', 'rep')
- new_mom_out: float32 [16, 1536, 768], P('exp', 'rep')
The draws below stay inside these ranges and needn't reach their ends.
Inputs may be any that keep to these rules, and one draw needn't show every extreme that they name: `routes`: within the 128 rows of one device and one inner step no expert is named by more than 32 rows, a bound that some block reaches; the two experts of a frame differ.
All inputs are finite; a program needn't handle non-finite values.
Results may differ from the reference program's by a relative error of at most 0.0075.
Values may be sent and summed in bfloat16 or wider, within the bound.
No kernel may reach another device: no remote copies, remote signals or barrier semaphores. Data moves between devices by JAX's collectives and lax.ppermute only.
A program may use at most 128 MiB of HBM per device.

```python
import math
import jax
import jax.numpy as jnp
import numpy as np
from jax import lax

D = 768
H = 1536
EXPERTS = 16
TOK_DEV = 128
STEPS = 2
CAP = 32
TOKENS = 2048
REPS = 16
N_EXP = 16


def levels(stream_key, shape, pieces, low, largest):
    loudness, own = 1.0, jax.random.fold_in(stream_key, 6)
    for axis_at, blocks in pieces:
        heights = jnp.exp(jax.random.uniform(jax.random.fold_in(own, axis_at), (blocks,), jnp.float32, low / len(pieces), largest / len(pieces)))
        loudness = loudness * jnp.repeat(heights, shape[axis_at] // blocks).reshape([-1 if axis == axis_at else 1 for axis in range(len(shape))])
    return loudness


def deal_out(stream_key, own, number, rows, amount, top, reach, skew):
    order = jax.random.permutation(stream_key, amount)
    crowded, common = load_shares(amount, rows * top, reach, skew, True), load_shares(amount, rows * top, reach, skew, False)
    places = jnp.arange(amount)

    def named(tallies, rotation):
        used = int((tallies > 0).sum())
        fixed = max(1, used // 4)
        shifted = fixed + (places - fixed + rotation * (used - fixed)) % max(1, amount - fixed)
        return jnp.zeros((amount,), jnp.int32).at[order[jnp.where(places < fixed, places, shifted)]].set(jnp.asarray(tallies, jnp.int32))

    tallies = jnp.where(number % 4 == 0, named(crowded, number // 4), named(common, number - number // 4 - 1))
    mixed = jax.random.permutation(jax.random.fold_in(own, 3), amount)
    donor, taker = mixed[0:amount // 2 * 2:2], mixed[1:amount // 2 * 2:2]
    slack = jnp.minimum(tallies[donor] - 1, reach - tallies[taker]) // 2
    slack = jnp.where((donor == order[0]) | (taker == order[0]) | (tallies[taker] == 0), 0, jnp.maximum(slack, 0))
    shifted = jax.random.randint(jax.random.fold_in(own, 4), (amount // 2,), 0, 1 << 20) % (slack + 1)
    tallies = tallies.at[donor].add(-shifted).at[taker].add(shifted)
    labels = jnp.searchsorted(jnp.cumsum(tallies), jnp.arange(rows * top), side="right").astype(jnp.int32)
    table = labels.reshape(top, rows).T
    table = table[jax.random.permutation(jax.random.fold_in(own, 1), rows)]
    rotation = jax.random.randint(jax.random.fold_in(own, 2), (rows, 1), 0, top)
    return jnp.take_along_axis(table, (jnp.arange(top)[None, :] + rotation) % top, axis=1)


def load_shares(number_of, total, bound, lean, full):
    loads = [(1 << 20) // math.isqrt(standing ** lean) + 1 for standing in range(1, number_of + 1)]
    largest = bound if full else min(bound, max(-(-total // number_of), total * loads[0] // sum(loads)))
    least = 1 if total - largest >= number_of - 1 else 0
    holding, surplus = [largest] + [least] * (number_of - 1), total - largest - least * (number_of - 1)
    while surplus > 0:
        candidates = [i for i in range(1, number_of) if holding[i] < largest] or [i for i in range(1, number_of) if holding[i] < bound]
        whole, budget = sum([loads[i] for i in candidates]), surplus
        for i in candidates:
            addition = min(bound - holding[i], max(1, budget * loads[i] // whole), surplus)
            holding[i] = holding[i] + addition
            surplus = surplus - addition
    return np.array(holding)


def noise(key, extent, width, bound, pieces=(), kind=jnp.bfloat16):
    array = width * jax.random.normal(key, extent, jnp.float32)
    if pieces:
        array = array * levels(key, extent, pieces, -0.22, 0.18)
    return jnp.clip(array, -bound, bound).astype(kind)


def setup_inputs(seed: int = 0) -> dict:
    key_of = jax.random.split(jax.random.key(seed), 9)
    w_in = noise(key_of[0], (EXPERTS, D, H), D ** -0.5, 0.21875, ((0, 16),))
    w_out = noise(key_of[1], (EXPERTS, H, D), H ** -0.5, 0.15625, ((0, 16),))
    mom_in = noise(key_of[2], (EXPERTS, D, H), 0.004, 0.024, ((0, 16), (1, 16)), jnp.float32)
    mom_out = noise(key_of[3], (EXPERTS, H, D), 0.004, 0.024, ((0, 16), (1, 16)), jnp.float32)
    frames = noise(key_of[4], (REPS, STEPS, TOKENS, D), 1.0, 6.0, ((0, 16), (2, 16)))
    targets = noise(key_of[5], (REPS, STEPS, TOKENS, D), 1.0, 6.0, ((0, 16), (2, 16)))
    routes_keys = jax.random.split(jax.random.fold_in(key_of[6], 1), REPS * STEPS * TOKENS // TOK_DEV)
    routes_turns = jax.random.permutation(jax.random.fold_in(key_of[6], 3), REPS * STEPS * TOKENS // TOK_DEV)
    routes = jax.vmap(lambda own, number: deal_out(jax.random.fold_in(key_of[6], 2), own, number, TOK_DEV, EXPERTS, 2, CAP, 1))(routes_keys, routes_turns).reshape((REPS, STEPS, TOKENS, 2))
    gates = jnp.clip(0.1 + 0.79999997 * jax.random.uniform(key_of[7], (REPS, STEPS, TOKENS, 2), jnp.float32) ** levels(key_of[7], (REPS, STEPS, TOKENS, 2), ((0, 16), (2, 16)), -0.2, 0.2), 0.1, 0.9)
    return {"w_in": w_in, "w_out": w_out, "mom_in": mom_in, "mom_out": mom_out, "frames": frames, "targets": targets, "routes": routes, "gates": gates}


def slot_table(route_rows):
    flat = route_rows.reshape(-1)
    onehot = (flat[:, None] == jnp.arange(EXPERTS, dtype=jnp.int32)[None, :]).astype(jnp.int32)
    running = jnp.cumsum(onehot, axis=0)
    return (lax.optimization_barrier(jnp.sum(running * onehot, axis=1)) - 1).reshape(route_rows.shape)

def adamw(theta, first, second, grad, count):
    first = 0.9 * first + 0.1 * grad
    second = 0.95 * second + 0.05 * grad * grad
    ratio = first / (1.0 - 0.9 ** count) / (jnp.sqrt(second / (1.0 - 0.95 ** count)) + 0.01)
    return (theta - 0.004 * (ratio + 0.1 * theta), first, second)

def as_bf16(theta):
    rounded = lax.optimization_barrier(theta.astype(jnp.bfloat16))
    return rounded.astype(jnp.float32)

def gradients(theta_in, theta_out, frame_rows, target_rows, route_rows, gate_rows):
    total = frame_rows.shape[0]
    source = jnp.broadcast_to((jnp.arange(total, dtype=jnp.int32) // TOK_DEV)[:, None], (total, 2))
    slot_rows = jax.vmap(slot_table)(route_rows.reshape(N_EXP, TOK_DEV, 2)).reshape(total, 2)
    spread = jnp.broadcast_to(frame_rows[:, None, :], (total, 2, D))
    buffer = jnp.zeros((EXPERTS, N_EXP, CAP, D), jnp.bfloat16).at[route_rows, source, slot_rows].set(spread)
    expert_rows = buffer.reshape(EXPERTS, N_EXP * CAP, D).astype(jnp.float32)
    first_w = as_bf16(theta_in)
    second_w = as_bf16(theta_out)
    hidden = jnp.einsum('erd,edh->erh', expert_rows, first_w)
    active = jax.nn.gelu(hidden).astype(jnp.bfloat16)
    produced = jnp.einsum('erh,ehd->erd', active.astype(jnp.float32), second_w).astype(jnp.bfloat16)
    produced = produced.reshape(EXPERTS, N_EXP, CAP, D)
    picked = produced[route_rows, source, slot_rows].astype(jnp.float32)
    combined = lax.optimization_barrier(jnp.sum(gate_rows[:, :, None] * picked, axis=1))
    residue = (combined - target_rows.astype(jnp.float32)) / TOK_DEV
    cotangent = (gate_rows[:, :, None] * residue[:, None, :]).astype(jnp.bfloat16)
    cot_buffer = jnp.zeros((EXPERTS, N_EXP, CAP, D), jnp.bfloat16).at[route_rows, source, slot_rows].set(cotangent)
    cot_rows = cot_buffer.reshape(EXPERTS, N_EXP * CAP, D).astype(jnp.float32)
    grad_out = jnp.einsum('erh,erd->ehd', active.astype(jnp.float32), cot_rows)
    upstream = jnp.einsum('erd,ehd->erh', cot_rows, second_w)
    _, pull = jax.vjp(jax.nn.gelu, hidden)
    local_grad, = pull(upstream)
    dh_rows = local_grad.astype(jnp.bfloat16).astype(jnp.float32)
    grad_in = jnp.einsum('erd,erh->edh', expert_rows, dh_rows)
    return (grad_in, grad_out)

def replica_delta(w_in, w_out, frame_r, target_r, route_r, gate_r):
    theta_in = w_in.astype(jnp.float32)
    theta_out = w_out.astype(jnp.float32)
    first_in = jnp.zeros_like(theta_in)
    second_in = jnp.zeros_like(theta_in)
    first_out = jnp.zeros_like(theta_out)
    second_out = jnp.zeros_like(theta_out)
    for inner_step in range(STEPS):
        grad_in, grad_out = gradients(theta_in, theta_out, frame_r[inner_step], target_r[inner_step], route_r[inner_step], gate_r[inner_step])
        theta_out, first_out, second_out = adamw(theta_out, first_out, second_out, grad_out, inner_step + 1)
        theta_in, first_in, second_in = adamw(theta_in, first_in, second_in, grad_in, inner_step + 1)
    return (w_in.astype(jnp.float32) - theta_in, w_out.astype(jnp.float32) - theta_out)

def reference(w_in, w_out, mom_in, mom_out, frames, targets, routes, gates):

    def accumulate(carry, items):
        delta_in, delta_out = replica_delta(w_in, w_out, items[0], items[1], items[2], items[3])
        return ((carry[0] + delta_in, carry[1] + delta_out), None)
    start = (jnp.zeros(w_in.shape, jnp.float32), jnp.zeros(w_out.shape, jnp.float32))
    (total_in, total_out), _ = lax.scan(accumulate, start, (frames, targets, routes, gates))
    delta_in = total_in / REPS
    delta_out = total_out / REPS
    new_mom_in = 0.9 * mom_in + delta_in
    new_mom_out = 0.9 * mom_out + delta_out
    new_w_in = (w_in.astype(jnp.float32) - 0.7 * (delta_in + 0.9 * new_mom_in)).astype(jnp.bfloat16)
    new_w_out = (w_out.astype(jnp.float32) - 0.7 * (delta_out + 0.9 * new_mom_out)).astype(jnp.bfloat16)
    return (new_w_in, new_w_out, new_mom_in, new_mom_out)
```

```python
import functools
import math

import jax
import jax.numpy as jnp
from jax import lax
from jax.experimental import pallas as pl
from jax.experimental.pallas import tpu as pltpu
from jax.sharding import PartitionSpec as P

F32 = jnp.float32
BF16 = jnp.bfloat16
MIB = 1 << 20
NX = 4
NZ = 4


def dot(left, right, on_left=1, on_right=0):
    return lax.dot_general(
        left, right, (((on_left,), (on_right,)), ((), ())), preferred_element_type=F32
    )


def places(routes, capacity):
    rows = routes.shape[0]
    first, second = routes[:, 0:1], routes[:, 1:2]
    lane = lax.broadcasted_iota(jnp.int32, (rows, 128), 1)
    names_first, names_second = lane == first, lane == second
    named = jnp.where(names_first | names_second, 1.0, 0.0).astype(BF16)
    earlier = lax.broadcasted_iota(jnp.int32, (rows, rows), 0) > lax.broadcasted_iota(
        jnp.int32, (rows, rows), 1
    )
    count = dot(jnp.where(earlier, 1.0, 0.0).astype(BF16), named)
    slot_first = jnp.sum(jnp.where(names_first, count, 0.0), axis=1, keepdims=True)
    slot_second = jnp.sum(jnp.where(names_second, count, 0.0), axis=1, keepdims=True)
    return (
        first * capacity + slot_first.astype(jnp.int32),
        second * capacity + slot_second.astype(jnp.int32),
    )


def one_hot(place, size):
    lane = lax.broadcasted_iota(jnp.int32, (place.shape[0], size), 1)
    return jnp.where(lane == place, 1.0, 0.0).astype(BF16)


def gelu_and_slope(x):
    c = math.sqrt(2.0 / math.pi)
    square = x * x
    bent = jnp.tanh(c * (x + 0.044715 * (square * x)))
    half = 0.5 * (1.0 + bent)
    slope = half + 0.5 * x * (1.0 - bent * bent) * (c * (1.0 + 3 * 0.044715 * square))
    return x * half, slope


def after_one(weight, grad):
    ratio = grad / (jnp.abs(grad) + 0.01)
    return weight - 0.004 * (ratio + 0.1 * weight)


def change_of_two(weight, grad_one, grad_two):
    theta = after_one(weight, grad_one)
    first = (0.09 / 0.19) * grad_one + (0.1 / 0.19) * grad_two
    second = (0.0475 / 0.0975) * (grad_one * grad_one) + (0.05 / 0.0975) * (grad_two * grad_two)
    ratio = first / (jnp.sqrt(second) + 0.01)
    return weight - (theta - 0.004 * (ratio + 0.1 * theta))


def params(limit=48):
    return pltpu.CompilerParams(vmem_limit_bytes=limit * MIB)


def cost(flops, size):
    return pl.CostEstimate(flops=int(flops), bytes_accessed=int(size), transcendentals=0)


def place_kernel(capacity, routes_ref, frames_ref, out_ref):
    size = out_ref.shape[0]
    first, second = places(routes_ref[...], capacity)
    spread = one_hot(first, size) + one_hot(second, size)
    out_ref[...] = dot(spread, frames_ref[...], 0, 0).astype(BF16)


def place_frames(routes, frames, size, capacity):
    return pl.pallas_call(
        functools.partial(place_kernel, capacity),
        out_shape=jax.ShapeDtypeStruct((size, frames.shape[1]), BF16),
        compiler_params=params(),
        cost_estimate=cost(2e8, 2e6),
        name="place_frames",
    )(routes, frames)


def residue_kernel(capacity, routes_ref, gates_ref, targets_ref, returned_ref, out_ref):
    size = out_ref.shape[0]
    rows = routes_ref.shape[0]
    first, second = places(routes_ref[...], capacity)
    hot_first, hot_second = one_hot(first, size), one_hot(second, size)
    gate_first, gate_second = gates_ref[:, 0:1], gates_ref[:, 1:2]
    returned = returned_ref[...]
    combined = gate_first * dot(hot_first, returned) + gate_second * dot(hot_second, returned)
    residue = (combined - targets_ref[...].astype(F32)) * (1.0 / rows)
    cot_first = (gate_first * residue).astype(BF16)
    cot_second = (gate_second * residue).astype(BF16)
    out_ref[...] = (dot(hot_first, cot_first, 0, 0) + dot(hot_second, cot_second, 0, 0)).astype(BF16)


def place_residue(routes, gates, targets, returned, capacity):
    return pl.pallas_call(
        functools.partial(residue_kernel, capacity),
        out_shape=jax.ShapeDtypeStruct(returned.shape, BF16),
        compiler_params=params(),
        cost_estimate=cost(4e8, 4e6),
        name="place_residue",
    )(routes, gates, targets, returned)


def forward_kernel(rows_ref, w_in_ref, w_out_ref, hidden_ref, active_ref, produced_ref, total):
    step = pl.program_id(0)
    hidden = dot(rows_ref[...], w_in_ref[...])
    hidden_ref[...] = hidden
    active = gelu_and_slope(hidden)[0].astype(BF16)
    active_ref[...] = active
    part = dot(active, w_out_ref[...])

    @pl.when(step == 0)
    def _():
        total[...] = part

    @pl.when(step > 0)
    def _():
        total[...] += part

    @pl.when(step == pl.num_programs(0) - 1)
    def _():
        produced_ref[...] = total[...].astype(BF16)


def forward(rows, w_in, w_out, tile=512):
    slots, width = rows.shape
    hid = w_in.shape[1]
    whole = pl.BlockSpec((slots, width), lambda i: (0, 0))
    by_col = pl.BlockSpec((slots, tile), lambda i: (0, i))
    return pl.pallas_call(
        forward_kernel,
        grid=(hid // tile,),
        in_specs=[
            whole,
            pl.BlockSpec((width, tile), lambda i: (0, i)),
            pl.BlockSpec((tile, width), lambda i: (i, 0)),
        ],
        out_specs=[by_col, by_col, whole],
        out_shape=[
            jax.ShapeDtypeStruct((slots, hid), F32),
            jax.ShapeDtypeStruct((slots, hid), BF16),
            jax.ShapeDtypeStruct((slots, width), BF16),
        ],
        scratch_shapes=[pltpu.VMEM((slots, width), F32)],
        compiler_params=params(),
        cost_estimate=cost(2.4e9, 1e7),
        name="forward",
    )(rows, w_in, w_out)


def turn_kernel(
    rows_ref,
    next_ref,
    cot_ref,
    w_in_ref,
    w_out_ref,
    hidden_ref,
    active_ref,
    dh_ref,
    theta_out_ref,
    hidden_next_ref,
    active_next_ref,
    produced_ref,
    total,
    turned,
):
    step = pl.program_id(0)

    @pl.when(step == 0)
    def _():
        turned[...] = rows_ref[...].T

    cot = cot_ref[...]
    w_out = w_out_ref[...]
    upstream = dot(cot, w_out, 1, 1)
    dh = (upstream * gelu_and_slope(hidden_ref[...])[1]).astype(BF16)
    dh_ref[...] = dh
    grad_in = dot(turned[...], dh)
    theta_in = after_one(w_in_ref[...].astype(F32), grad_in).astype(BF16)
    hidden = dot(next_ref[...], theta_in)
    hidden_next_ref[...] = hidden
    grad_out = dot(active_ref[...], cot, 0, 0)
    theta_out = after_one(w_out.astype(F32), grad_out).astype(BF16)
    theta_out_ref[...] = theta_out
    active = gelu_and_slope(hidden)[0].astype(BF16)
    active_next_ref[...] = active
    part = dot(active, theta_out)

    @pl.when(step == 0)
    def _():
        total[...] = part

    @pl.when(step > 0)
    def _():
        total[...] += part

    @pl.when(step == pl.num_programs(0) - 1)
    def _():
        produced_ref[...] = total[...].astype(BF16)


def turn(rows, next_rows, cot, w_in, w_out, hidden, active, tile=256):
    slots, width = rows.shape
    hid = w_in.shape[1]
    whole = pl.BlockSpec((slots, width), lambda i: (0, 0))
    by_col = pl.BlockSpec((slots, tile), lambda i: (0, i))
    by_row = pl.BlockSpec((tile, width), lambda i: (i, 0))
    return pl.pallas_call(
        turn_kernel,
        grid=(hid // tile,),
        in_specs=[
            whole,
            whole,
            whole,
            pl.BlockSpec((width, tile), lambda i: (0, i)),
            by_row,
            by_col,
            by_col,
        ],
        out_specs=[by_col, by_row, by_col, by_col, whole],
        out_shape=[
            jax.ShapeDtypeStruct((slots, hid), BF16),
            jax.ShapeDtypeStruct((hid, width), BF16),
            jax.ShapeDtypeStruct((slots, hid), F32),
            jax.ShapeDtypeStruct((slots, hid), BF16),
            jax.ShapeDtypeStruct((slots, width), BF16),
        ],
        scratch_shapes=[pltpu.VMEM((slots, width), F32), pltpu.VMEM((width, slots), BF16)],
        compiler_params=params(),
        cost_estimate=cost(7e9, 2e7),
        name="turn",
    )(rows, next_rows, cot, w_in, w_out, hidden, active)


PARTS = {
    0: (("own", 0), ("own", 2)),
    1: (("far_plus", 2), ("near_plus", 0)),
    2: (("far_minus", 0), ("far_plus", 0)),
    3: (("near_minus", 0), ("far_minus", 2)),
}
PART_SHARDS = {"far_minus": 4, "far_plus": 4, "near_minus": 2, "near_plus": 2, "own": 4}
HALVES = ((1, 3), (0, 2))


def store_change(rep, band, w_ref, grad_one, grad_two, outs):
    x, z = rep % NX, rep // NX
    for k in range(NX):
        for half, members in enumerate(HALVES):
            name, at = PARTS[k][half]
            for i, m in enumerate(members):
                first = pl.multiple_of((jnp.bitwise_xor(z, m) * NX + (x + k) % NX) * band, 16)
                rows = pl.ds(first, band)
                change = change_of_two(w_ref[rows, :].astype(F32), grad_one[rows, :], grad_two[rows, :])
                outs[name][at + i] = change.astype(BF16)


def change_out_kernel(rep_ref, w_ref, act_one, cot_one, act_two, cot_two, *rest):
    outs = dict(zip(PART_SHARDS, rest[:5]))
    grad_one, grad_two = rest[5:]
    grad_one[...] = dot(act_one[...], cot_one[...], 0, 0)
    grad_two[...] = dot(act_two[...], cot_two[...], 0, 0)
    band = outs["own"].shape[1]
    store_change(rep_ref[0], band, w_ref, grad_one, grad_two, outs)


def change_out(rep, replicas, w_out, act_one, cot_one, act_two, cot_two, tile=256):
    slots, hid = act_one.shape
    width = cot_one.shape[1]
    band = hid // replicas
    act = pl.BlockSpec((slots, hid), lambda i: (0, 0))
    cot = pl.BlockSpec((slots, tile), lambda i: (0, i))
    return pl.pallas_call(
        change_out_kernel,
        grid=(width // tile,),
        in_specs=[
            pl.BlockSpec(memory_space=pltpu.SMEM),
            pl.BlockSpec((hid, tile), lambda i: (0, i)),
            act,
            cot,
            act,
            cot,
        ],
        out_specs=[pl.BlockSpec((n, band, tile), lambda i: (0, 0, i)) for n in PART_SHARDS.values()],
        out_shape=[jax.ShapeDtypeStruct((n, band, width), BF16) for n in PART_SHARDS.values()],
        scratch_shapes=[pltpu.VMEM((hid, tile), F32), pltpu.VMEM((hid, tile), F32)],
        compiler_params=params(),
        cost_estimate=cost(2.4e9, 1e7),
        name="change_out",
    )(rep, w_out, act_one, cot_one, act_two, cot_two)


def change_in_kernel(
    rep_ref, w_ref, rows_one, dh_one, rows_two, cot_two, theta_out, hidden_two, *rest
):
    outs = dict(zip(PART_SHARDS, rest[:5]))
    grad_one, grad_two, turned_one, turned_two = rest[5:]

    @pl.when(pl.program_id(0) == 0)
    def _():
        turned_one[...] = rows_one[...].T
        turned_two[...] = rows_two[...].T

    upstream = dot(cot_two[...], theta_out[...], 1, 1)
    dh_two = (upstream * gelu_and_slope(hidden_two[...])[1]).astype(BF16)
    grad_one[...] = dot(turned_one[...], dh_one[...])
    grad_two[...] = dot(turned_two[...], dh_two)
    band = outs["own"].shape[1]
    store_change(rep_ref[0], band, w_ref, grad_one, grad_two, outs)


def change_in(rep, replicas, w_in, rows_one, dh_one, rows_two, cot_two, theta_out, hidden_two, tile=256):
    slots, hid = dh_one.shape
    width = rows_one.shape[1]
    band = width // replicas
    whole = pl.BlockSpec((slots, width), lambda i: (0, 0))
    by_col = pl.BlockSpec((slots, tile), lambda i: (0, i))
    return pl.pallas_call(
        change_in_kernel,
        grid=(hid // tile,),
        in_specs=[
            pl.BlockSpec(memory_space=pltpu.SMEM),
            pl.BlockSpec((width, tile), lambda i: (0, i)),
            whole,
            by_col,
            whole,
            whole,
            pl.BlockSpec((tile, width), lambda i: (i, 0)),
            by_col,
        ],
        out_specs=[pl.BlockSpec((n, band, tile), lambda i: (0, 0, i)) for n in PART_SHARDS.values()],
        out_shape=[jax.ShapeDtypeStruct((n, band, hid), BF16) for n in PART_SHARDS.values()],
        scratch_shapes=[
            pltpu.VMEM((width, tile), F32),
            pltpu.VMEM((width, tile), F32),
            pltpu.VMEM((width, slots), BF16),
            pltpu.VMEM((width, slots), BF16),
        ],
        compiler_params=params(),
        cost_estimate=cost(3.6e9, 1.5e7),
        name="change_in",
    )(rep, w_in, rows_one, dh_one, rows_two, cot_two, theta_out, hidden_two)


def rep_permutation(step_x, flip_z):
    pairs = []
    for z in range(NZ):
        for x in range(NX):
            pairs.append((z * NX + x, (z ^ flip_z) * NX + (x + step_x) % NX))
    return pairs


def shift_x(array, step):
    return lax.ppermute(array, "rep", rep_permutation(step, 0))


def swap_z(array, flip):
    return lax.ppermute(array, "rep", rep_permutation(0, flip))


def add(*terms):
    return sum(term.astype(F32) for term in terms)


def reduce_to_owner(parts):
    far_minus, far_plus, near_minus, near_plus, own = parts
    from_plus = shift_x(far_minus, -1)
    from_minus = shift_x(far_plus, 1)
    last_plus = shift_x(add(near_minus, from_plus[:2]).astype(BF16), -1)
    last_minus = shift_x(add(near_plus, from_minus[:2]).astype(BF16), 1)
    half_a = add(own[:2], from_minus[2:], last_plus).astype(BF16)
    other = swap_z(half_a, 1)
    half_b = add(own[2:], from_plus[2:], last_minus)
    mine = half_b + other.astype(F32)
    across = swap_z(mine[1].astype(BF16), 2)
    return mine[0] + across.astype(F32)


def assemble_kernel(rep_ref, home, plus, minus, cross_a, cross_b, out, sem):
    x, z = rep_ref[0] % NX, rep_ref[0] // NX
    band = home.shape[1]
    copies = []
    for k, source in ((0, home), (1, plus), (3, minus), (2, None)):
        for m in range(NZ):
            if source is None:
                half = cross_a if m < 2 else cross_b
                block = half.at[m % 2]
            else:
                block = source.at[m]
            first = pl.multiple_of((jnp.bitwise_xor(z, m) * NX + (x + k) % NX) * band, 16)
            copies.append(pltpu.make_async_copy(block, out.at[pl.ds(first, band), :], sem.at[len(copies)]))
    for copy in copies:
        copy.start()
    for copy in copies:
        copy.wait()


def gather_from_owner(rep, own):
    band, columns = own.shape
    pair = jnp.stack([own, swap_z(own, 2)])
    other = swap_z(pair, 1)
    home = jnp.stack([pair[0], other[0], pair[1], other[1]])
    minus = shift_x(home, 1)
    plus = shift_x(home, -1)
    cross_a = shift_x(minus[:2], 1)
    cross_b = shift_x(plus[2:], -1)
    any_spec = pl.BlockSpec(memory_space=pl.ANY)
    return pl.pallas_call(
        assemble_kernel,
        in_specs=[pl.BlockSpec(memory_space=pltpu.SMEM)] + [any_spec] * 5,
        out_specs=any_spec,
        out_shape=jax.ShapeDtypeStruct((NZ * NX * band, columns), BF16),
        scratch_shapes=[pltpu.SemaphoreType.DMA((NZ * NX,))],
        cost_estimate=cost(0, 5e6),
        name="assemble",
    )(rep, home, plus, minus, cross_a, cross_b)


def outer_update(rep, start_w, momentum, summed, replicas):
    averaged = summed / replicas
    new_momentum = 0.9 * momentum + averaged
    rows = momentum.shape[0]
    own_rows = lax.dynamic_slice_in_dim(start_w, rep * rows, rows, 0).astype(F32)
    return (own_rows - 0.7 * (averaged + 0.9 * new_momentum)).astype(BF16), new_momentum


def exchange(rows, experts):
    slots, width = rows.shape
    block = rows.reshape(experts, slots // experts, width)
    return lax.all_to_all(block, "exp", split_axis=0, concat_axis=0, tiled=True).reshape(slots, width)


def per_device(w_in, w_out, mom_in, mom_out, frames, targets, routes, gates):
    experts = lax.axis_size("exp")
    replicas = lax.axis_size("rep")
    rep = lax.axis_index("rep")
    rep_ref = rep.reshape(1).astype(jnp.int32)
    capacity = 4 * frames.shape[2] // experts
    slots = experts * capacity
    w_in, w_out, mom_in, mom_out = w_in[0], w_out[0], mom_in[0], mom_out[0]
    frames, targets, routes, gates = frames[0], targets[0], routes[0], gates[0]

    rows_one = exchange(place_frames(routes[0], frames[0], slots, capacity), experts)
    hidden_one, active_one, produced = forward(rows_one, w_in, w_out)
    rows_two = exchange(place_frames(routes[1], frames[1], slots, capacity), experts)
    returned = exchange(produced, experts)
    cot_one = exchange(place_residue(routes[0], gates[0], targets[0], returned, capacity), experts)
    dh_one, theta_out, hidden_two, active_two, produced = turn(
        rows_one, rows_two, cot_one, w_in, w_out, hidden_one, active_one
    )
    returned = exchange(produced, experts)
    cot_two = exchange(place_residue(routes[1], gates[1], targets[1], returned, capacity), experts)

    parts_out = change_out(rep_ref, replicas, w_out, active_one, cot_one, active_two, cot_two)
    parts_in = change_in(
        rep_ref, replicas, w_in, rows_one, dh_one, rows_two, cot_two, theta_out, hidden_two
    )
    summed_out = reduce_to_owner(parts_out)
    summed_in = reduce_to_owner(parts_in)
    part_out, new_mom_out = outer_update(rep, w_out, mom_out, summed_out, replicas)
    new_w_out = gather_from_owner(rep_ref, part_out)
    part_in, new_mom_in = outer_update(rep, w_in, mom_in, summed_in, replicas)
    new_w_in = gather_from_owner(rep_ref, part_in)
    return (new_w_in[None], new_w_out[None], new_mom_in[None], new_mom_out[None])


def solution(mesh):
    in_specs = (
        P("exp", None, None),
        P("exp", None, None),
        P("exp", "rep", None),
        P("exp", "rep", None),
        P("rep", None, "exp", None),
        P("rep", None, "exp", None),
        P("rep", None, "exp", None),
        P("rep", None, "exp", None),
    )
    out_specs = (
        P("exp", None, None),
        P("exp", None, None),
        P("exp", "rep", None),
        P("exp", "rep", None),
    )
    return jax.shard_map(
        per_device, mesh=mesh, in_specs=in_specs, out_specs=out_specs, check_vma=False
    )
```

```python
import functools
import math

import jax
import jax.numpy as jnp
from jax import lax
from jax.experimental import pallas as pl
from jax.experimental.pallas import tpu as pltpu
from jax.sharding import PartitionSpec as P

F32 = jnp.float32
BF16 = jnp.bfloat16
MIB = 1 << 20
NX = 4
NZ = 4


def dot(left, right, on_left=1, on_right=0):
    return lax.dot_general(
        left, right, (((on_left,), (on_right,)), ((), ())), preferred_element_type=F32
    )


def places(routes, capacity):
    rows = routes.shape[0]
    first, second = routes[:, 0:1], routes[:, 1:2]
    lane = lax.broadcasted_iota(jnp.int32, (rows, 128), 1)
    names_first, names_second = lane == first, lane == second
    named = jnp.where(names_first | names_second, 1.0, 0.0).astype(BF16)
    earlier = lax.broadcasted_iota(jnp.int32, (rows, rows), 0) > lax.broadcasted_iota(
        jnp.int32, (rows, rows), 1
    )
    count = dot(jnp.where(earlier, 1.0, 0.0).astype(BF16), named)
    slot_first = jnp.sum(jnp.where(names_first, count, 0.0), axis=1, keepdims=True)
    slot_second = jnp.sum(jnp.where(names_second, count, 0.0), axis=1, keepdims=True)
    return (
        first * capacity + slot_first.astype(jnp.int32),
        second * capacity + slot_second.astype(jnp.int32),
    )


def one_hot(place, size):
    lane = lax.broadcasted_iota(jnp.int32, (place.shape[0], size), 1)
    return jnp.where(lane == place, 1.0, 0.0).astype(BF16)


def gelu_and_slope(x):
    c = math.sqrt(2.0 / math.pi)
    square = x * x
    bent = jnp.tanh(c * (x + 0.044715 * (square * x)))
    half = 0.5 * (1.0 + bent)
    slope = half + 0.5 * x * (1.0 - bent * bent) * (c * (1.0 + 3 * 0.044715 * square))
    return x * half, slope


RATE, DECAY = 0.004, 0.1
KEEP = 1.0 - RATE * DECAY


def after_one(weight, grad):
    return KEEP * weight - RATE * (grad * pl.reciprocal(jnp.abs(grad) + 0.01))


def change_of_two(weight, grad_one, grad_two):
    first = (0.09 / 0.19) * grad_one + (0.1 / 0.19) * grad_two
    second = (0.0475 / 0.0975) * (grad_one * grad_one) + (0.05 / 0.0975) * (grad_two * grad_two)
    below_two = second * lax.rsqrt(second + 1e-30) + 0.01
    below_one = jnp.abs(grad_one) + 0.01
    over = KEEP * (grad_one * below_two) + first * below_one
    return (1.0 - KEEP * KEEP) * weight + RATE * (over * pl.reciprocal(below_one * below_two))


def params(limit=48):
    return pltpu.CompilerParams(vmem_limit_bytes=limit * MIB)


def cost(flops, size):
    return pl.CostEstimate(flops=int(flops), bytes_accessed=int(size), transcendentals=0)


def place_kernel(capacity, routes_ref, frames_ref, out_ref):
    size = out_ref.shape[0]
    first, second = places(routes_ref[...], capacity)
    spread = one_hot(first, size) + one_hot(second, size)
    out_ref[...] = dot(spread, frames_ref[...], 0, 0).astype(BF16)


def place_frames(routes, frames, size, capacity):
    return pl.pallas_call(
        functools.partial(place_kernel, capacity),
        out_shape=jax.ShapeDtypeStruct((size, frames.shape[1]), BF16),
        compiler_params=params(),
        cost_estimate=cost(2e8, 2e6),
        name="place_frames",
    )(routes, frames)


def residue_kernel(capacity, routes_ref, gates_ref, targets_ref, returned_ref, out_ref):
    size = out_ref.shape[0]
    rows = routes_ref.shape[0]
    first, second = places(routes_ref[...], capacity)
    hot_first, hot_second = one_hot(first, size), one_hot(second, size)
    gate_first, gate_second = gates_ref[:, 0:1], gates_ref[:, 1:2]
    returned = returned_ref[...]
    combined = gate_first * dot(hot_first, returned) + gate_second * dot(hot_second, returned)
    residue = (combined - targets_ref[...].astype(F32)) * (1.0 / rows)
    cot_first = (gate_first * residue).astype(BF16)
    cot_second = (gate_second * residue).astype(BF16)
    out_ref[...] = (dot(hot_first, cot_first, 0, 0) + dot(hot_second, cot_second, 0, 0)).astype(BF16)


def place_residue(routes, gates, targets, returned, capacity):
    return pl.pallas_call(
        functools.partial(residue_kernel, capacity),
        out_shape=jax.ShapeDtypeStruct(returned.shape, BF16),
        compiler_params=params(),
        cost_estimate=cost(4e8, 4e6),
        name="place_residue",
    )(routes, gates, targets, returned)


def forward_kernel(rows_ref, w_in_ref, w_out_ref, hidden_ref, active_ref, produced_ref, total):
    step = pl.program_id(0)
    hidden = dot(rows_ref[...], w_in_ref[...])
    hidden_ref[...] = hidden
    active = gelu_and_slope(hidden)[0].astype(BF16)
    active_ref[...] = active
    part = dot(active, w_out_ref[...])

    @pl.when(step == 0)
    def _():
        total[...] = part

    @pl.when(step > 0)
    def _():
        total[...] += part

    @pl.when(step == pl.num_programs(0) - 1)
    def _():
        produced_ref[...] = total[...].astype(BF16)


def forward(rows, w_in, w_out, tile=512):
    slots, width = rows.shape
    hid = w_in.shape[1]
    whole = pl.BlockSpec((slots, width), lambda i: (0, 0))
    by_col = pl.BlockSpec((slots, tile), lambda i: (0, i))
    return pl.pallas_call(
        forward_kernel,
        grid=(hid // tile,),
        in_specs=[
            whole,
            pl.BlockSpec((width, tile), lambda i: (0, i)),
            pl.BlockSpec((tile, width), lambda i: (i, 0)),
        ],
        out_specs=[by_col, by_col, whole],
        out_shape=[
            jax.ShapeDtypeStruct((slots, hid), F32),
            jax.ShapeDtypeStruct((slots, hid), BF16),
            jax.ShapeDtypeStruct((slots, width), BF16),
        ],
        scratch_shapes=[pltpu.VMEM((slots, width), F32)],
        compiler_params=params(),
        cost_estimate=cost(7e9, 1e7),
        name="forward",
    )(rows, w_in, w_out)


def turn_kernel(
    rows_ref,
    next_ref,
    cot_ref,
    w_in_ref,
    w_out_ref,
    hidden_ref,
    active_ref,
    dh_ref,
    theta_out_ref,
    hidden_next_ref,
    active_next_ref,
    produced_ref,
    total,
    turned,
):
    step = pl.program_id(0)

    @pl.when(step == 0)
    def _():
        turned[...] = rows_ref[...].T

    cot = cot_ref[...]
    w_out = w_out_ref[...]
    upstream = dot(cot, w_out, 1, 1)
    dh = (upstream * gelu_and_slope(hidden_ref[...])[1]).astype(BF16)
    dh_ref[...] = dh
    grad_in = dot(turned[...], dh)
    theta_in = after_one(w_in_ref[...].astype(F32), grad_in).astype(BF16)
    hidden = dot(next_ref[...], theta_in)
    hidden_next_ref[...] = hidden
    grad_out = dot(active_ref[...], cot, 0, 0)
    theta_out = after_one(w_out.astype(F32), grad_out).astype(BF16)
    theta_out_ref[...] = theta_out
    active = gelu_and_slope(hidden)[0].astype(BF16)
    active_next_ref[...] = active
    part = dot(active, theta_out)

    @pl.when(step == 0)
    def _():
        total[...] = part

    @pl.when(step > 0)
    def _():
        total[...] += part

    @pl.when(step == pl.num_programs(0) - 1)
    def _():
        produced_ref[...] = total[...].astype(BF16)


def turn(rows, next_rows, cot, w_in, w_out, hidden, active, tile=256):
    slots, width = rows.shape
    hid = w_in.shape[1]
    whole = pl.BlockSpec((slots, width), lambda i: (0, 0))
    by_col = pl.BlockSpec((slots, tile), lambda i: (0, i))
    by_row = pl.BlockSpec((tile, width), lambda i: (i, 0))
    return pl.pallas_call(
        turn_kernel,
        grid=(hid // tile,),
        in_specs=[
            whole,
            whole,
            whole,
            pl.BlockSpec((width, tile), lambda i: (0, i)),
            by_row,
            by_col,
            by_col,
        ],
        out_specs=[by_col, by_row, by_col, by_col, whole],
        out_shape=[
            jax.ShapeDtypeStruct((slots, hid), BF16),
            jax.ShapeDtypeStruct((hid, width), BF16),
            jax.ShapeDtypeStruct((slots, hid), F32),
            jax.ShapeDtypeStruct((slots, hid), BF16),
            jax.ShapeDtypeStruct((slots, width), BF16),
        ],
        scratch_shapes=[pltpu.VMEM((slots, width), F32), pltpu.VMEM((width, slots), BF16)],
        compiler_params=params(),
        cost_estimate=cost(1.5e10, 2e7),
        name="turn",
    )(rows, next_rows, cot, w_in, w_out, hidden, active)


PARTS = {
    0: (("own", 0), ("own", 2)),
    1: (("far_plus", 2), ("near_plus", 0)),
    2: (("far_minus", 0), ("far_plus", 0)),
    3: (("near_minus", 0), ("far_minus", 2)),
}
PART_SHARDS = {"far_minus": 4, "far_plus": 4, "near_minus": 2, "near_plus": 2, "own": 4}
HALVES = ((1, 3), (0, 2))


def store_band(k, m, rows, w_ref, grad_one, grad_two, outs):
    half = 0 if m in HALVES[0] else 1
    name, at = PARTS[k][half]
    change = change_of_two(w_ref[rows, :].astype(F32), grad_one[rows, :], grad_two[rows, :])
    outs[name][at + HALVES[half].index(m)] = change.astype(BF16)


def change_out_kernel(rep_ref, w_ref, act_one, cot_one, act_two, cot_two, *rest):
    outs = dict(zip(PART_SHARDS, rest[:5]))
    grad_one, grad_two = rest[5:]
    grad_one[...] = dot(act_one[...], cot_one[...], 0, 0)
    grad_two[...] = dot(act_two[...], cot_two[...], 0, 0)
    band = outs["own"].shape[1]
    x = rep_ref[0] % NX
    for m in range(NZ):

        @pl.when(pl.program_id(0) == m)
        def _():
            for k in range(NX):
                rows = pl.ds(pl.multiple_of((x + k) % NX * band, 16), band)
                store_band(k, m, rows, w_ref, grad_one, grad_two, outs)


def change_out(rep, replicas, w_out, act_one, cot_one, act_two, cot_two):
    slots, hid = act_one.shape
    width = cot_one.shape[1]
    band = hid // replicas
    tile = band * NX

    def z_of(i, rep_ref):
        return jnp.bitwise_xor(rep_ref[0] // NX, i)

    act = pl.BlockSpec((slots, tile), lambda i, r: (0, z_of(i, r)))
    cot = pl.BlockSpec((slots, width), lambda i, r: (0, 0))
    return pl.pallas_call(
        change_out_kernel,
        grid_spec=pltpu.PrefetchScalarGridSpec(
            num_scalar_prefetch=1,
            grid=(NZ,),
            in_specs=[
                pl.BlockSpec((tile, width), lambda i, r: (z_of(i, r), 0)),
                act,
                cot,
                act,
                cot,
            ],
            out_specs=[
                pl.BlockSpec((n, band, width), lambda i, r: (0, 0, 0)) for n in PART_SHARDS.values()
            ],
            scratch_shapes=[pltpu.VMEM((tile, width), F32), pltpu.VMEM((tile, width), F32)],
        ),
        out_shape=[jax.ShapeDtypeStruct((n, band, width), BF16) for n in PART_SHARDS.values()],
        compiler_params=params(),
        cost_estimate=cost(8e9, 1e7),
        name="change_out",
    )(rep, w_out, act_one, cot_one, act_two, cot_two)


def change_in_kernel(
    rep_ref, w_ref, rows_one, dh_one, rows_two, cot_two, theta_out, hidden_two, *rest
):
    outs = dict(zip(PART_SHARDS, rest[:5]))
    grad_one, grad_two, turned_one, turned_two = rest[5:]

    @pl.when(pl.program_id(0) == 0)
    def _():
        turned_one[...] = rows_one[...].T
        turned_two[...] = rows_two[...].T

    upstream = dot(cot_two[...], theta_out[...], 1, 1)
    dh_two = (upstream * gelu_and_slope(hidden_two[...])[1]).astype(BF16)
    grad_one[...] = dot(turned_one[...], dh_one[...])
    grad_two[...] = dot(turned_two[...], dh_two)
    band = outs["own"].shape[1]
    x, z = rep_ref[0] % NX, rep_ref[0] // NX
    for k in range(NX):
        for m in range(NZ):
            first = pl.multiple_of((jnp.bitwise_xor(z, m) * NX + (x + k) % NX) * band, 16)
            store_band(k, m, pl.ds(first, band), w_ref, grad_one, grad_two, outs)


def change_in(rep, replicas, w_in, rows_one, dh_one, rows_two, cot_two, theta_out, hidden_two, tile=256):
    slots, hid = dh_one.shape
    width = rows_one.shape[1]
    band = width // replicas
    whole = pl.BlockSpec((slots, width), lambda i: (0, 0))
    by_col = pl.BlockSpec((slots, tile), lambda i: (0, i))
    return pl.pallas_call(
        change_in_kernel,
        grid=(hid // tile,),
        in_specs=[
            pl.BlockSpec(memory_space=pltpu.SMEM),
            pl.BlockSpec((width, tile), lambda i: (0, i)),
            whole,
            by_col,
            whole,
            whole,
            pl.BlockSpec((tile, width), lambda i: (i, 0)),
            by_col,
        ],
        out_specs=[pl.BlockSpec((n, band, tile), lambda i: (0, 0, i)) for n in PART_SHARDS.values()],
        out_shape=[jax.ShapeDtypeStruct((n, band, hid), BF16) for n in PART_SHARDS.values()],
        scratch_shapes=[
            pltpu.VMEM((width, tile), F32),
            pltpu.VMEM((width, tile), F32),
            pltpu.VMEM((width, slots), BF16),
            pltpu.VMEM((width, slots), BF16),
        ],
        compiler_params=params(),
        cost_estimate=cost(1.2e10, 1.5e7),
        name="change_in",
    )(rep, w_in, rows_one, dh_one, rows_two, cot_two, theta_out, hidden_two)


def rep_permutation(step_x, flip_z):
    pairs = []
    for z in range(NZ):
        for x in range(NX):
            pairs.append((z * NX + x, (z ^ flip_z) * NX + (x + step_x) % NX))
    return pairs


def shift_x(array, step):
    return lax.ppermute(array, "rep", rep_permutation(step, 0))


def swap_z(array, flip):
    return lax.ppermute(array, "rep", rep_permutation(0, flip))


def add(*terms):
    return sum(term.astype(F32) for term in terms)


def reduce_to_owner(parts):
    far_minus, far_plus, near_minus, near_plus, own = parts
    from_plus = shift_x(far_minus, -1)
    from_minus = shift_x(far_plus, 1)
    last_plus = shift_x(add(near_minus, from_plus[:2]).astype(BF16), -1)
    last_minus = shift_x(add(near_plus, from_minus[:2]).astype(BF16), 1)
    half_a = add(own[:2], from_minus[2:], last_plus).astype(BF16)
    other = swap_z(half_a, 1)
    half_b = add(own[2:], from_plus[2:], last_minus)
    mine = half_b + other.astype(F32)
    across = swap_z(mine[1].astype(BF16), 2)
    return mine[0] + across.astype(F32)


def assemble_kernel(rep_ref, home, plus, minus, cross_a, cross_b, out):
    x, z = rep_ref[0] % NX, rep_ref[0] // NX
    band = home.shape[1]
    for k in range(NX):
        for m in range(NZ):
            if k == 2:
                block = (cross_a if m < 2 else cross_b)[m % 2]
            else:
                block = (home, plus, None, minus)[k][m]
            first = pl.multiple_of((jnp.bitwise_xor(z, m) * NX + (x + k) % NX) * band, 16)
            out[pl.ds(first, band), :] = block


def gather_from_owner(rep, own):
    band, columns = own.shape
    pair = jnp.stack([own, swap_z(own, 2)])
    other = swap_z(pair, 1)
    home = jnp.stack([pair[0], other[0], pair[1], other[1]])
    minus = shift_x(home, 1)
    plus = shift_x(home, -1)
    cross_a = shift_x(minus[:2], 1)
    cross_b = shift_x(plus[2:], -1)
    tile = 384

    def part(shards):
        return pl.BlockSpec((shards, band, tile), lambda i: (0, 0, i))

    rows = NZ * NX * band
    return pl.pallas_call(
        assemble_kernel,
        grid=(columns // tile,),
        in_specs=[pl.BlockSpec(memory_space=pltpu.SMEM)] + [part(n) for n in (4, 4, 4, 2, 2)],
        out_specs=pl.BlockSpec((rows, tile), lambda i: (0, i)),
        out_shape=jax.ShapeDtypeStruct((rows, columns), BF16),
        compiler_params=params(),
        cost_estimate=cost(0, 5e6),
        name="assemble",
    )(rep, home, plus, minus, cross_a, cross_b)


def outer_update(rep, start_w, momentum, summed, replicas):
    averaged = summed / replicas
    new_momentum = 0.9 * momentum + averaged
    rows = momentum.shape[0]
    own_rows = lax.dynamic_slice_in_dim(start_w, rep * rows, rows, 0).astype(F32)
    return (own_rows - 0.7 * (averaged + 0.9 * new_momentum)).astype(BF16), new_momentum


def exchange(rows, experts):
    slots, width = rows.shape
    block = rows.reshape(experts, slots // experts, width)
    return lax.all_to_all(block, "exp", split_axis=0, concat_axis=0, tiled=True).reshape(slots, width)


def per_device(w_in, w_out, mom_in, mom_out, frames, targets, routes, gates):
    experts = lax.axis_size("exp")
    replicas = lax.axis_size("rep")
    rep = lax.axis_index("rep")
    rep_ref = rep.reshape(1).astype(jnp.int32)
    capacity = 4 * frames.shape[2] // experts
    slots = experts * capacity
    w_in, w_out, mom_in, mom_out = w_in[0], w_out[0], mom_in[0], mom_out[0]
    frames, targets, routes, gates = frames[0], targets[0], routes[0], gates[0]

    rows_one = exchange(place_frames(routes[0], frames[0], slots, capacity), experts)
    hidden_one, active_one, produced = forward(rows_one, w_in, w_out)
    rows_two = exchange(place_frames(routes[1], frames[1], slots, capacity), experts)
    returned = exchange(produced, experts)
    cot_one = exchange(place_residue(routes[0], gates[0], targets[0], returned, capacity), experts)
    dh_one, theta_out, hidden_two, active_two, produced = turn(
        rows_one, rows_two, cot_one, w_in, w_out, hidden_one, active_one
    )
    returned = exchange(produced, experts)
    cot_two = exchange(place_residue(routes[1], gates[1], targets[1], returned, capacity), experts)

    parts_out = change_out(rep_ref, replicas, w_out, active_one, cot_one, active_two, cot_two)
    parts_in = change_in(
        rep_ref, replicas, w_in, rows_one, dh_one, rows_two, cot_two, theta_out, hidden_two
    )
    summed_out = reduce_to_owner(parts_out)
    summed_in = reduce_to_owner(parts_in)
    part_out, new_mom_out = outer_update(rep, w_out, mom_out, summed_out, replicas)
    new_w_out = gather_from_owner(rep_ref, part_out)
    part_in, new_mom_in = outer_update(rep, w_in, mom_in, summed_in, replicas)
    new_w_in = gather_from_owner(rep_ref, part_in)
    return (new_w_in[None], new_w_out[None], new_mom_in[None], new_mom_out[None])


def solution(mesh):
    in_specs = (
        P("exp", None, None),
        P("exp", None, None),
        P("exp", "rep", None),
        P("exp", "rep", None),
        P("rep", None, "exp", None),
        P("rep", None, "exp", None),
        P("rep", None, "exp", None),
        P("rep", None, "exp", None),
    )
    out_specs = (
        P("exp", None, None),
        P("exp", None, None),
        P("exp", "rep", None),
        P("exp", "rep", None),
    )
    return jax.shard_map(
        per_device, mesh=mesh, in_specs=in_specs, out_specs=out_specs, check_vma=False
    )
```

```python
import functools
import math

import jax
import jax.numpy as jnp
from jax import lax
from jax.experimental import pallas as pl
from jax.experimental.pallas import tpu as pltpu
from jax.sharding import PartitionSpec as P

F32 = jnp.float32
BF16 = jnp.bfloat16
MIB = 1 << 20
NX = 4
NZ = 4


SMEM_SPEC = pl.BlockSpec(memory_space=pltpu.SMEM)
VMEM_SPEC = pl.BlockSpec(memory_space=pltpu.VMEM)
ANY_SPEC = pl.BlockSpec(memory_space=pl.ANY)


def dot(left, right, on_left=1, on_right=0):
    return lax.dot_general(
        left, right, (((on_left,), (on_right,)), ((), ())), preferred_element_type=F32
    )


def places(routes, capacity):
    rows = routes.shape[0]
    first, second = routes[:, 0:1], routes[:, 1:2]
    lane = lax.broadcasted_iota(jnp.int32, (rows, 128), 1)
    names_first, names_second = lane == first, lane == second
    named = jnp.where(names_first | names_second, 1.0, 0.0).astype(BF16)
    earlier = lax.broadcasted_iota(jnp.int32, (rows, rows), 0) > lax.broadcasted_iota(
        jnp.int32, (rows, rows), 1
    )
    count = dot(jnp.where(earlier, 1.0, 0.0).astype(BF16), named)
    slot_first = jnp.sum(jnp.where(names_first, count, 0.0), axis=1, keepdims=True)
    slot_second = jnp.sum(jnp.where(names_second, count, 0.0), axis=1, keepdims=True)
    return (
        first * capacity + slot_first.astype(jnp.int32),
        second * capacity + slot_second.astype(jnp.int32),
    )


def one_hot(place, size):
    lane = lax.broadcasted_iota(jnp.int32, (place.shape[0], size), 1)
    return jnp.where(lane == place, 1.0, 0.0).astype(BF16)


def gelu_and_slope(x):
    c = math.sqrt(2.0 / math.pi)
    square = x * x
    bent = jnp.tanh(c * (x + 0.044715 * (square * x)))
    half = 0.5 * (1.0 + bent)
    slope = half + 0.5 * x * (1.0 - bent * bent) * (c * (1.0 + 3 * 0.044715 * square))
    return x * half, slope


RATE, DECAY = 0.004, 0.1
KEEP = 1.0 - RATE * DECAY


def inverse(x):
    near = pl.reciprocal(x, approx=True)
    return near * (2.0 - x * near)


def after_one(weight, grad):
    return KEEP * weight - RATE * (grad * inverse(jnp.abs(grad) + 0.01))


def change_of_two(weight, grad_one, grad_two):
    first = (0.09 / 0.19) * grad_one + (0.1 / 0.19) * grad_two
    second = (0.0475 / 0.0975) * (grad_one * grad_one) + (0.05 / 0.0975) * (grad_two * grad_two)
    below_two = second * lax.rsqrt(second + 1e-30) + 0.01
    below_one = jnp.abs(grad_one) + 0.01
    over = KEEP * (grad_one * below_two) + first * below_one
    return (1.0 - KEEP * KEEP) * weight + RATE * (over * inverse(below_one * below_two))


def params(limit=48):
    return pltpu.CompilerParams(vmem_limit_bytes=limit * MIB)


def cost(flops, size):
    return pl.CostEstimate(flops=int(flops), bytes_accessed=int(size), transcendentals=0)


def place_kernel(capacity, routes_ref, frames_ref, out_ref):
    experts, _, width = out_ref.shape
    size = experts * capacity
    for step in range(routes_ref.shape[0]):
        first, second = places(routes_ref[step], capacity)
        spread = one_hot(first, size) + one_hot(second, size)
        placed = dot(spread, frames_ref[step], 0, 0).astype(BF16)
        out_ref[:, step * capacity : (step + 1) * capacity, :] = placed.reshape(
            experts, capacity, width
        )


def place_frames(routes, frames, experts, capacity):
    steps, _, width = frames.shape
    return pl.pallas_call(
        functools.partial(place_kernel, capacity),
        out_shape=jax.ShapeDtypeStruct((experts, steps * capacity, width), BF16),
        compiler_params=params(),
        cost_estimate=cost(2e9, 3e6),
        name="place_frames",
    )(routes, frames)


def residue_kernel(capacity, routes_ref, gates_ref, targets_ref, returned_ref, out_ref):
    size = out_ref.shape[0]
    rows = routes_ref.shape[0]
    first, second = places(routes_ref[...], capacity)
    hot_first, hot_second = one_hot(first, size), one_hot(second, size)
    gate_first, gate_second = gates_ref[:, 0:1], gates_ref[:, 1:2]
    returned = returned_ref[...]
    combined = gate_first * dot(hot_first, returned) + gate_second * dot(hot_second, returned)
    residue = (combined - targets_ref[...].astype(F32)) * (1.0 / rows)
    cot_first = (gate_first * residue).astype(BF16)
    cot_second = (gate_second * residue).astype(BF16)
    out_ref[...] = (dot(hot_first, cot_first, 0, 0) + dot(hot_second, cot_second, 0, 0)).astype(BF16)


def place_residue(routes, gates, targets, returned, capacity):
    return pl.pallas_call(
        functools.partial(residue_kernel, capacity),
        out_shape=jax.ShapeDtypeStruct(returned.shape, BF16),
        compiler_params=params(),
        cost_estimate=cost(4e8, 4e6),
        name="place_residue",
    )(routes, gates, targets, returned)


def flat(ref):
    return ref[...].reshape(-1, ref.shape[-1])


def rows_of(step, experts, capacity, width):
    return pl.BlockSpec((experts, capacity, width), lambda i: (0, step, 0))


def forward_kernel(rows_ref, w_in_ref, w_out_ref, slope_ref, active_ref, produced_ref, total):
    step = pl.program_id(0)
    active, slope_ref[...] = gelu_and_slope(dot(flat(rows_ref), w_in_ref[...]))
    active = active.astype(BF16)
    active_ref[...] = active
    part = dot(active, w_out_ref[...])

    @pl.when(step == 0)
    def _():
        total[...] = part

    @pl.when(step > 0)
    def _():
        total[...] += part

    @pl.when(step == pl.num_programs(0) - 1)
    def _():
        produced_ref[...] = total[...].astype(BF16)


def forward(rows, capacity, w_in, w_out, tile=512):
    experts, _, width = rows.shape
    slots = experts * capacity
    hid = w_in.shape[1]
    whole = pl.BlockSpec((slots, width), lambda i: (0, 0))
    by_col = pl.BlockSpec((slots, tile), lambda i: (0, i))
    return pl.pallas_call(
        forward_kernel,
        grid=(hid // tile,),
        in_specs=[
            rows_of(0, experts, capacity, width),
            pl.BlockSpec((width, tile), lambda i: (0, i)),
            pl.BlockSpec((tile, width), lambda i: (i, 0)),
        ],
        out_specs=[by_col, by_col, whole],
        out_shape=[
            jax.ShapeDtypeStruct((slots, hid), F32),
            jax.ShapeDtypeStruct((slots, hid), BF16),
            jax.ShapeDtypeStruct((slots, width), BF16),
        ],
        scratch_shapes=[pltpu.VMEM((slots, width), F32)],
        compiler_params=params(58),
        cost_estimate=cost(7e9, 1e7),
        name="forward",
    )(rows, w_in, w_out)


SUB = 256


def turn_kernel(
    rows_ref,
    next_ref,
    cot_ref,
    w_in_ref,
    w_out_ref,
    slope_ref,
    active_ref,
    dh_ref,
    theta_out_ref,
    slope_next_ref,
    active_next_ref,
    produced_ref,
    total,
    turned,
):
    step = pl.program_id(0)

    @pl.when(step == 0)
    def _():
        turned[...] = flat(rows_ref).T

    cot = cot_ref[...]
    tile = w_in_ref.shape[1]
    part = 0.0
    for at in range(0, tile, SUB):
        cols = slice(at, at + SUB)
        w_out = w_out_ref[cols, :]
        dh = (dot(cot, w_out, 1, 1) * slope_ref[:, cols]).astype(BF16)
        dh_ref[:, cols] = dh
        grad_in = dot(turned[...], dh)
        theta_in = after_one(w_in_ref[:, cols].astype(F32), grad_in).astype(BF16)
        grad_out = dot(active_ref[:, cols], cot, 0, 0)
        theta_out = after_one(w_out.astype(F32), grad_out).astype(BF16)
        theta_out_ref[cols, :] = theta_out
        active, slope_next_ref[:, cols] = gelu_and_slope(dot(flat(next_ref), theta_in))
        active = active.astype(BF16)
        active_next_ref[:, cols] = active
        part += dot(active, theta_out)

    @pl.when(step == 0)
    def _():
        total[...] = part

    @pl.when(step > 0)
    def _():
        total[...] += part

    @pl.when(step == pl.num_programs(0) - 1)
    def _():
        produced_ref[...] = total[...].astype(BF16)


def turn(rows, capacity, cot, w_in, w_out, slope, active, tile=512):
    experts, _, width = rows.shape
    slots = experts * capacity
    hid = w_in.shape[1]
    whole = pl.BlockSpec((slots, width), lambda i: (0, 0))
    by_col = pl.BlockSpec((slots, tile), lambda i: (0, i))
    by_row = pl.BlockSpec((tile, width), lambda i: (i, 0))
    return pl.pallas_call(
        turn_kernel,
        grid=(hid // tile,),
        in_specs=[
            rows_of(0, experts, capacity, width),
            rows_of(1, experts, capacity, width),
            whole,
            pl.BlockSpec((width, tile), lambda i: (0, i)),
            by_row,
            by_col,
            by_col,
        ],
        out_specs=[by_col, by_row, by_col, by_col, whole],
        out_shape=[
            jax.ShapeDtypeStruct((slots, hid), BF16),
            jax.ShapeDtypeStruct((hid, width), BF16),
            jax.ShapeDtypeStruct((slots, hid), F32),
            jax.ShapeDtypeStruct((slots, hid), BF16),
            jax.ShapeDtypeStruct((slots, width), BF16),
        ],
        scratch_shapes=[pltpu.VMEM((slots, width), F32), pltpu.VMEM((width, slots), BF16)],
        compiler_params=params(58),
        cost_estimate=cost(1.5e10, 2e7),
        name="turn",
    )(rows, rows, cot, w_in, w_out, slope, active)


PARTS = {
    0: (("own", 0), ("own", 2)),
    1: (("far_plus", 2), ("near_plus", 0)),
    2: (("far_minus", 0), ("far_plus", 0)),
    3: (("near_minus", 0), ("far_minus", 2)),
}
PART_SHARDS = {"far_minus": 4, "far_plus": 4, "near_minus": 2, "near_plus": 2, "own": 4}
HALVES = ((1, 3), (0, 2))


def store_band(k, m, rows, w_ref, grad_one, grad_two, outs):
    half = 0 if m in HALVES[0] else 1
    name, at = PARTS[k][half]
    change = change_of_two(w_ref[rows, :].astype(F32), grad_one[rows, :], grad_two[rows, :])
    outs[name][at + HALVES[half].index(m)] = change.astype(BF16)


def change_out_kernel(rep_ref, w_ref, act_one, cot_one, act_two, cot_two, *rest):
    outs = dict(zip(PART_SHARDS, rest[:5]))
    grad_one, grad_two = rest[5:]
    grad_one[...] = dot(act_one[...], cot_one[...], 0, 0)
    grad_two[...] = dot(act_two[...], cot_two[...], 0, 0)
    band = outs["own"].shape[1]
    x = rep_ref[0] % NX
    for m in range(NZ):

        @pl.when(pl.program_id(0) == m)
        def _():
            for k in range(NX):
                rows = pl.ds(pl.multiple_of((x + k) % NX * band, 16), band)
                store_band(k, m, rows, w_ref, grad_one, grad_two, outs)


def change_out(rep, replicas, w_out, act_one, cot_one, act_two, cot_two):
    slots, hid = act_one.shape
    width = cot_one.shape[1]
    band = hid // replicas
    tile = band * NX

    def z_of(i, rep_ref):
        return jnp.bitwise_xor(rep_ref[0] // NX, i)

    act = pl.BlockSpec((slots, tile), lambda i, r: (0, z_of(i, r)))
    cot = pl.BlockSpec((slots, width), lambda i, r: (0, 0))
    return pl.pallas_call(
        change_out_kernel,
        grid_spec=pltpu.PrefetchScalarGridSpec(
            num_scalar_prefetch=1,
            grid=(NZ,),
            in_specs=[
                pl.BlockSpec((tile, width), lambda i, r: (z_of(i, r), 0)),
                act,
                cot,
                act,
                cot,
            ],
            out_specs=[
                pl.BlockSpec((n, band, width), lambda i, r: (0, 0, 0)) for n in PART_SHARDS.values()
            ],
            scratch_shapes=[pltpu.VMEM((tile, width), F32), pltpu.VMEM((tile, width), F32)],
        ),
        out_shape=[jax.ShapeDtypeStruct((n, band, width), BF16) for n in PART_SHARDS.values()],
        compiler_params=params(48),
        cost_estimate=cost(8e9, 1e7),
        name="change_out",
    )(rep, w_out, act_one, cot_one, act_two, cot_two)


def change_in_kernel(
    rep_ref, w_ref, rows_one, dh_one, rows_two, cot_two, theta_out, slope_two, *rest
):
    outs = dict(zip(PART_SHARDS, rest[:5]))
    grad_one, grad_two, turned_one, turned_two = rest[5:]

    @pl.when(pl.program_id(0) == 0)
    def _():
        turned_one[...] = flat(rows_one).T
        turned_two[...] = flat(rows_two).T

    upstream = dot(cot_two[...], theta_out[...], 1, 1)
    dh_two = (upstream * slope_two[...]).astype(BF16)
    grad_one[...] = dot(turned_one[...], dh_one[...])
    grad_two[...] = dot(turned_two[...], dh_two)
    band = outs["own"].shape[1]
    x, z = rep_ref[0] % NX, rep_ref[0] // NX
    for k in range(NX):
        for m in range(NZ):
            first = pl.multiple_of((jnp.bitwise_xor(z, m) * NX + (x + k) % NX) * band, 16)
            store_band(k, m, pl.ds(first, band), w_ref, grad_one, grad_two, outs)


def change_in(rep, replicas, rows, capacity, w_in, dh_one, cot_two, theta_out, slope_two, tile=256):
    slots, hid = dh_one.shape
    experts, _, width = rows.shape
    band = width // replicas
    whole = pl.BlockSpec((slots, width), lambda i: (0, 0))
    by_col = pl.BlockSpec((slots, tile), lambda i: (0, i))
    return pl.pallas_call(
        change_in_kernel,
        grid=(hid // tile,),
        in_specs=[
            SMEM_SPEC,
            pl.BlockSpec((width, tile), lambda i: (0, i)),
            rows_of(0, experts, capacity, width),
            by_col,
            rows_of(1, experts, capacity, width),
            whole,
            pl.BlockSpec((tile, width), lambda i: (i, 0)),
            by_col,
        ],
        out_specs=[pl.BlockSpec((n, band, tile), lambda i: (0, 0, i)) for n in PART_SHARDS.values()],
        out_shape=[jax.ShapeDtypeStruct((n, band, hid), BF16) for n in PART_SHARDS.values()],
        scratch_shapes=[
            pltpu.VMEM((width, tile), F32),
            pltpu.VMEM((width, tile), F32),
            pltpu.VMEM((width, slots), BF16),
            pltpu.VMEM((width, slots), BF16),
        ],
        compiler_params=params(48),
        cost_estimate=cost(1.2e10, 1.5e7),
        name="change_in",
    )(rep, w_in, rows, dh_one, rows, cot_two, theta_out, slope_two)


def rep_permutation(step_x, flip_z):
    pairs = []
    for z in range(NZ):
        for x in range(NX):
            pairs.append((z * NX + x, (z ^ flip_z) * NX + (x + step_x) % NX))
    return pairs


def shift_x(array, step):
    return lax.ppermute(array, "rep", rep_permutation(step, 0))


def swap_z(array, flip):
    return lax.ppermute(array, "rep", rep_permutation(0, flip))


def small_call(kernel, out_shape, name, in_specs, *operands, **more):
    return pl.pallas_call(
        kernel,
        in_specs=in_specs,
        out_specs=jax.tree.map(lambda _: VMEM_SPEC, out_shape),
        out_shape=out_shape,
        compiler_params=params(),
        cost_estimate=cost(1e3, 1e3),
        name=name,
        **more,
    )(*operands)


def near_kernel(near_minus, near_plus, from_plus, from_minus, *refs):
    to_minus, to_plus = refs[-2:]
    to_minus[...] = (near_minus[...].astype(F32) + from_plus[:2].astype(F32)).astype(BF16)
    to_plus[...] = (near_plus[...].astype(F32) + from_minus[:2].astype(F32)).astype(BF16)


def sum_kernel(held, own, from_plus, from_minus, last_plus, last_minus, *refs):
    outs = refs[2 * held :]
    for half, members in enumerate(HALVES):
        for i, m in enumerate(members):
            total = own[2 * half + i].astype(F32)
            if half == 0:
                total += from_minus[2 + i].astype(F32) + last_plus[i].astype(F32)
            else:
                total += from_plus[2 + i].astype(F32) + last_minus[i].astype(F32)
            outs[m][...] = total.astype(outs[m].dtype)


def start_far(parts):
    return shift_x(parts[0], -1), shift_x(parts[1], 1)


def near_sums(parts, far, after):
    return small_call(
        near_kernel,
        [jax.ShapeDtypeStruct(parts[2].shape, BF16)] * 2,
        "near",
        [VMEM_SPEC] * 4 + [ANY_SPEC],
        parts[2],
        parts[3],
        *far,
        after,
    )


def owner_terms(parts, far, near, held):
    band_shape = parts[4].shape[1:]
    last = shift_x(near[0], -1), shift_x(near[1], 1)
    out = pl.pallas_call(
        functools.partial(sum_kernel, len(held)),
        in_specs=[VMEM_SPEC] * 5 + [ANY_SPEC] * len(held),
        out_specs=[ANY_SPEC] * len(held) + [VMEM_SPEC] * NZ,
        out_shape=[jax.ShapeDtypeStruct(a.shape, BF16) for a in held]
        + [jax.ShapeDtypeStruct(band_shape, F32 if m == 0 else BF16) for m in range(NZ)],
        input_output_aliases={5 + i: i for i in range(len(held))},
        compiler_params=params(),
        cost_estimate=cost(1e3, 1e3),
        name="sums",
    )(parts[4], *far, *last, *held)
    return out[len(held) :], out[: len(held)]


def reduce_z(terms):
    return [terms[0]] + [swap_z(terms[m], m) for m in range(1, NZ)]


def update_kernel(replicas, me_ref, w_ref, mom_ref, *refs):
    new_w, new_mom = refs[NZ:]
    summed = refs[0][...]
    for term in refs[1:NZ]:
        summed += term[...].astype(F32)
    averaged = summed * (1.0 / replicas)
    momentum = 0.9 * mom_ref[...] + averaged
    new_mom[...] = momentum
    new_w[...] = (w_ref[...].astype(F32) - 0.7 * (averaged + 0.9 * momentum)).astype(BF16)


def outer_update(rep, replicas, w, momentum, terms):
    band, columns = momentum.shape
    whole = pl.BlockSpec((band, columns), lambda i, r: (0, 0))
    return pl.pallas_call(
        functools.partial(update_kernel, replicas),
        grid_spec=pltpu.PrefetchScalarGridSpec(
            num_scalar_prefetch=1,
            grid=(1,),
            in_specs=[pl.BlockSpec((band, columns), lambda i, r: (r[0], 0))] + [whole] * (1 + NZ),
            out_specs=[whole] * 2,
        ),
        out_shape=[
            jax.ShapeDtypeStruct((band, columns), BF16),
            jax.ShapeDtypeStruct((band, columns), F32),
        ],
        compiler_params=params(),
        cost_estimate=cost(1e3, 1e3),
        name="update",
    )(rep, w, momentum, *terms)


def stack_kernel(one, two, three, four, low, high):
    low[0], low[1], high[0], high[1] = one[...], two[...], three[...], four[...]


def assemble_kernel(rep_ref, *refs):
    out = refs[-1]
    x, z = rep_ref[0] % NX, rep_ref[0] // NX
    band = refs[0].shape[1]
    for k in range(NX):
        for m in range(NZ):
            first = pl.multiple_of((jnp.bitwise_xor(z, m) * NX + (x + k) % NX) * band, 16)
            out[pl.ds(first, band), :] = refs[2 * k + m // 2][m % 2]


def gather_from_owner(rep, own):
    band, columns = own.shape
    others = [swap_z(own, m) for m in range(1, NZ)]
    low, high = small_call(
        stack_kernel,
        [jax.ShapeDtypeStruct((2, band, columns), BF16)] * 2,
        "stack",
        [VMEM_SPEC] * NZ,
        own,
        *others,
    )
    low_minus, high_plus = shift_x(low, 1), shift_x(high, -1)
    high_minus, low_plus = shift_x(high, 1), shift_x(low, -1)
    low_cross, high_cross = shift_x(low_minus, 1), shift_x(high_plus, -1)
    tile = 384
    part = pl.BlockSpec((2, band, tile), lambda i: (0, 0, i))
    rows = NZ * NX * band
    return pl.pallas_call(
        assemble_kernel,
        grid=(columns // tile,),
        in_specs=[SMEM_SPEC] + [part] * 8,
        out_specs=pl.BlockSpec((rows, tile), lambda i: (0, i)),
        out_shape=jax.ShapeDtypeStruct((rows, columns), BF16),
        compiler_params=params(),
        cost_estimate=cost(1e3, 1e3),
        name="assemble",
    )(rep, low, high, low_plus, high_plus, low_cross, high_cross, low_minus, high_minus)


def exchange(rows, experts):
    slots, width = rows.shape
    block = rows.reshape(experts, slots // experts, width)
    return lax.all_to_all(block, "exp", split_axis=0, concat_axis=0, tiled=True).reshape(slots, width)


def per_device(w_in, w_out, mom_in, mom_out, frames, targets, routes, gates):
    experts = lax.axis_size("exp")
    replicas = lax.axis_size("rep")
    rep = lax.axis_index("rep")
    rep_ref = rep.reshape(1).astype(jnp.int32)
    capacity = 4 * frames.shape[2] // experts
    slots = experts * capacity
    w_in, w_out, mom_in, mom_out = w_in[0], w_out[0], mom_in[0], mom_out[0]
    frames, targets, routes, gates = frames[0], targets[0], routes[0], gates[0]

    rows = lax.all_to_all(
        place_frames(routes, frames, experts, capacity), "exp", split_axis=0, concat_axis=0, tiled=True
    )
    slope_one, active_one, produced = forward(rows, capacity, w_in, w_out)
    returned = exchange(produced, experts)
    cot_one = exchange(place_residue(routes[0], gates[0], targets[0], returned, capacity), experts)
    dh_one, theta_out, slope_two, active_two, produced = turn(
        rows, capacity, cot_one, w_in, w_out, slope_one, active_one
    )
    returned = exchange(produced, experts)
    cot_two = exchange(place_residue(routes[1], gates[1], targets[1], returned, capacity), experts)

    parts_out = change_out(rep_ref, replicas, w_out, active_one, cot_one, active_two, cot_two)
    far_out = start_far(parts_out)
    parts_in = change_in(
        rep_ref, replicas, rows, capacity, w_in, dh_one, cot_two, theta_out, slope_two
    )
    near_out = near_sums(parts_out, far_out, parts_in[4])
    terms_out, held = owner_terms(parts_out, far_out, near_out, parts_in[:2])
    parts_in = [*held, *parts_in[2:]]
    far_in = start_far(parts_in)
    terms_out = reduce_z(terms_out)
    near_in = near_sums(parts_in, far_in, parts_in[4])
    terms_in = reduce_z(owner_terms(parts_in, far_in, near_in, [])[0])
    part_out, new_mom_out = outer_update(rep_ref, replicas, w_out, mom_out, terms_out)
    new_w_out = gather_from_owner(rep_ref, part_out)
    part_in, new_mom_in = outer_update(rep_ref, replicas, w_in, mom_in, terms_in)
    new_w_in = gather_from_owner(rep_ref, part_in)
    return (new_w_in[None], new_w_out[None], new_mom_in[None], new_mom_out[None])


def solution(mesh):
    in_specs = (
        P("exp", None, None),
        P("exp", None, None),
        P("exp", "rep", None),
        P("exp", "rep", None),
        P("rep", None, "exp", None),
        P("rep", None, "exp", None),
        P("rep", None, "exp", None),
        P("rep", None, "exp", None),
    )
    out_specs = (
        P("exp", None, None),
        P("exp", None, None),
        P("exp", "rep", None),
        P("exp", "rep", None),
    )
    return jax.shard_map(
        per_device, mesh=mesh, in_specs=in_specs, out_specs=out_specs, check_vma=False
    )
```

```python
import functools
import math

import jax
import jax.numpy as jnp
from jax import lax
from jax.experimental import pallas as pl
from jax.experimental.pallas import tpu as pltpu
from jax.sharding import PartitionSpec as P

F32 = jnp.float32
BF16 = jnp.bfloat16
MIB = 1 << 20
NX = 4
NZ = 4
NY = 4


SMEM_SPEC = pl.BlockSpec(memory_space=pltpu.SMEM)
VMEM_SPEC = pl.BlockSpec(memory_space=pltpu.VMEM)
ANY_SPEC = pl.BlockSpec(memory_space=pl.ANY)


def dot(left, right, on_left=1, on_right=0):
    return lax.dot_general(
        left, right, (((on_left,), (on_right,)), ((), ())), preferred_element_type=F32
    )


def slots_of(first, second):
    rows = first.shape[0]
    lane = lax.broadcasted_iota(jnp.int32, (rows, 128), 1)
    names_first, names_second = lane == first, lane == second
    named = jnp.where(names_first | names_second, 1.0, 0.0).astype(BF16)
    earlier = lax.broadcasted_iota(jnp.int32, (rows, rows), 0) > lax.broadcasted_iota(
        jnp.int32, (rows, rows), 1
    )
    count = dot(jnp.where(earlier, 1.0, 0.0).astype(BF16), named)
    slot_first = jnp.sum(jnp.where(names_first, count, 0.0), axis=1, keepdims=True)
    slot_second = jnp.sum(jnp.where(names_second, count, 0.0), axis=1, keepdims=True)
    return slot_first.astype(jnp.int32), slot_second.astype(jnp.int32)


def places(routes, capacity):
    first, second = routes[:, 0:1], routes[:, 1:2]
    slot_first, slot_second = slots_of(first, second)
    return first * capacity + slot_first, second * capacity + slot_second


def one_hot(place, size):
    lane = lax.broadcasted_iota(jnp.int32, (place.shape[0], size), 1)
    return jnp.where(lane == place, 1.0, 0.0).astype(BF16)


def gelu_and_slope(x):
    c = math.sqrt(2.0 / math.pi)
    square = x * x
    bent = jnp.tanh(c * (x + 0.044715 * (square * x)))
    half = 0.5 * (1.0 + bent)
    slope = half + 0.5 * x * (1.0 - bent * bent) * (c * (1.0 + 3 * 0.044715 * square))
    return x * half, slope


RATE, DECAY = 0.004, 0.1
KEEP = 1.0 - RATE * DECAY


def inverse(x):
    near = pl.reciprocal(x, approx=True)
    return near * (2.0 - x * near)


def after_one(weight, grad):
    return KEEP * weight - RATE * (grad * inverse(jnp.abs(grad) + 0.01))


def first_part(weight, grad_one):
    ratio = grad_one * inverse(jnp.abs(grad_one) + 0.01)
    return (1.0 - KEEP * KEEP) * weight + (RATE * KEEP) * ratio


def second_part(grad_one, grad_two):
    first = (0.09 / 0.19) * grad_one + (0.1 / 0.19) * grad_two
    second = (0.0475 / 0.0975) * (grad_one * grad_one) + (0.05 / 0.0975) * (grad_two * grad_two)
    return RATE * (first * inverse(second * lax.rsqrt(second + 1e-30) + 0.01))


def change_of_two(weight, grad_one, grad_two):
    first = (0.09 / 0.19) * grad_one + (0.1 / 0.19) * grad_two
    second = (0.0475 / 0.0975) * (grad_one * grad_one) + (0.05 / 0.0975) * (grad_two * grad_two)
    below_two = second * lax.rsqrt(second + 1e-30) + 0.01
    below_one = jnp.abs(grad_one) + 0.01
    over = KEEP * (grad_one * below_two) + first * below_one
    return (1.0 - KEEP * KEEP) * weight + RATE * (over * inverse(below_one * below_two))


def params(limit=48):
    return pltpu.CompilerParams(vmem_limit_bytes=limit * MIB)


def cost(flops, size):
    return pl.CostEstimate(flops=int(flops), bytes_accessed=int(size), transcendentals=0)


def small_call(kernel, out_shape, name, in_specs, *operands, **more):
    return pl.pallas_call(
        kernel,
        in_specs=in_specs,
        out_specs=jax.tree.map(lambda _: VMEM_SPEC, out_shape),
        out_shape=out_shape,
        compiler_params=params(),
        cost_estimate=cost(1e3, 1e3),
        name=name,
        **more,
    )(*operands)


def place_kernel(capacity, routes_ref, frames_ref, out_ref):
    experts, _, width = out_ref.shape
    size = experts * capacity
    first, second = places(routes_ref[...], capacity)
    spread = one_hot(first, size) + one_hot(second, size)
    placed = dot(spread, frames_ref[...], 0, 0).astype(BF16)
    out_ref[...] = placed.reshape(experts, capacity, width)


def place_frames(routes, frames, experts, capacity):
    return pl.pallas_call(
        functools.partial(place_kernel, capacity),
        out_shape=jax.ShapeDtypeStruct((experts, capacity, frames.shape[1]), BF16),
        compiler_params=params(),
        cost_estimate=cost(2e9, 3e6),
        name="place_frames",
    )(routes, frames)


def spread_kernel(capacity, me_ref, routes_a, a_ref, routes_b, b_ref, *outs):
    me = me_ref[1]
    for block, (routes_ref, rows_ref) in enumerate(((routes_a, a_ref), (routes_b, b_ref))):
        routes = routes_ref[...].T.astype(jnp.int32)
        pair = routes[:, 0:1], routes[:, 1:2]
        hot = 0.0
        for expert, slot in zip(pair, slots_of(*pair)):
            ahead = jnp.bitwise_and((expert >> 2) - (me >> 2), NY - 1)
            here = jnp.bitwise_and(expert, 3) == jnp.bitwise_and(me, 3)
            hot += one_hot(jnp.where(here, ahead * capacity + slot, -1), NY * capacity)
        placed = dot(hot, rows_ref[...], 0, 0).astype(BF16)
        for ahead, out in enumerate(outs):
            out[block * capacity : (block + 1) * capacity, :] = placed[
                ahead * capacity : (ahead + 1) * capacity
            ]


def spread_rows(capacity, me, *blocks):
    width = blocks[1].shape[1]
    return small_call(
        functools.partial(spread_kernel, capacity),
        [jax.ShapeDtypeStruct((2 * capacity, width), BF16)] * NY,
        "spread_rows",
        [SMEM_SPEC] + [VMEM_SPEC] * 4,
        me,
        *blocks,
    )


def over_exp(array, along_y=0, flip_z=0, flip_core=0):
    pairs = []
    for y in range(NY):
        for z in range(2):
            for core in range(2):
                target = ((y + along_y) % NY, z ^ flip_z, core ^ flip_core)
                pairs.append((y * 4 + z * 2 + core, target[0] * 4 + target[1] * 2 + target[2]))
    return lax.ppermute(array, "exp", pairs)


def hold(arrays, after):
    return pl.pallas_call(
        lambda *refs: None,
        in_specs=[ANY_SPEC] * (len(arrays) + len(after)),
        out_specs=[ANY_SPEC] * len(arrays),
        out_shape=[jax.ShapeDtypeStruct(a.shape, a.dtype) for a in arrays],
        input_output_aliases={i: i for i in range(len(arrays))},
        cost_estimate=cost(1e3, 1e3),
        name="hold",
    )(*arrays, *after)


def dispatch(capacity, me, routes, own, cross_routes, cross):
    near = spread_rows(
        capacity, me, routes, own, over_exp(routes, flip_core=1), over_exp(own, flip_core=1)
    )
    far = spread_rows(
        capacity,
        me,
        cross_routes,
        cross,
        over_exp(cross_routes, flip_core=1),
        over_exp(cross, flip_core=1),
    )
    return [
        over_exp(piece, along_y=i) if i else piece for side in (near, far) for i, piece in enumerate(side)
    ]


def line_up(me, pieces, out):
    capacity = pieces[0].shape[0] // 2
    for at, piece in enumerate(pieces):
        for block in range(2):
            y = jnp.bitwise_and((me >> 2) - at % NY, NY - 1)
            place_of = jnp.bitwise_xor(jnp.bitwise_and(me, 3), 2 * (at // NY) + block)
            first = pl.multiple_of((y * 4 + place_of) * capacity, 32)
            out[pl.ds(first, capacity), :] = piece[block * capacity : (block + 1) * capacity, :]


def residue_kernel(capacity, routes_ref, gates_ref, targets_ref, returned_ref, *refs):
    out_ref = refs[-1]
    size = out_ref.shape[0]
    rows = routes_ref.shape[0]
    first, second = places(routes_ref[...], capacity)
    hot_first, hot_second = one_hot(first, size), one_hot(second, size)
    gate_first, gate_second = gates_ref[:, 0:1], gates_ref[:, 1:2]
    returned = returned_ref[...]
    combined = gate_first * dot(hot_first, returned) + gate_second * dot(hot_second, returned)
    residue = (combined - targets_ref[...].astype(F32)) * (1.0 / rows)
    cot_first = (gate_first * residue).astype(BF16)
    cot_second = (gate_second * residue).astype(BF16)
    out_ref[...] = (dot(hot_first, cot_first, 0, 0) + dot(hot_second, cot_second, 0, 0)).astype(BF16)


def place_residue(routes, gates, targets, returned, capacity, after=()):
    return small_call(
        functools.partial(residue_kernel, capacity),
        jax.ShapeDtypeStruct(returned.shape, BF16),
        "place_residue",
        [VMEM_SPEC] * 4 + [ANY_SPEC] * len(after),
        routes,
        gates,
        targets,
        returned,
        *after,
    )


def flat(ref):
    return ref[...].reshape(-1, ref.shape[-1])


def rows_spec(shape):
    return pl.BlockSpec(shape, lambda i: (0, 0, 0))


def forward_kernel(rows_ref, w_in_ref, w_out_ref, *refs):
    slope_ref, active_ref, produced_ref, total = refs[-4:]
    step = pl.program_id(0)
    active, slope_ref[...] = gelu_and_slope(dot(flat(rows_ref), w_in_ref[...]))
    active = active.astype(BF16)
    active_ref[...] = active
    part = dot(active, w_out_ref[...])

    @pl.when(step == 0)
    def _():
        total[...] = part

    @pl.when(step > 0)
    def _():
        total[...] += part

    @pl.when(step == pl.num_programs(0) - 1)
    def _():
        produced_ref[...] = total[...].astype(BF16)


def forward(rows, w_in, w_out, after, tile=512):
    experts, capacity, width = rows.shape
    slots = experts * capacity
    hid = w_in.shape[1]
    whole = pl.BlockSpec((slots, width), lambda i: (0, 0))
    by_col = pl.BlockSpec((slots, tile), lambda i: (0, i))
    return pl.pallas_call(
        forward_kernel,
        grid=(hid // tile,),
        in_specs=[
            rows_spec(rows.shape),
            pl.BlockSpec((width, tile), lambda i: (0, i)),
            pl.BlockSpec((tile, width), lambda i: (i, 0)),
        ]
        + [ANY_SPEC] * len(after),
        out_specs=[by_col, by_col, whole],
        out_shape=[
            jax.ShapeDtypeStruct((slots, hid), F32),
            jax.ShapeDtypeStruct((slots, hid), BF16),
            jax.ShapeDtypeStruct((slots, width), BF16),
        ],
        scratch_shapes=[pltpu.VMEM((slots, width), F32)],
        compiler_params=params(58),
        cost_estimate=cost(7e9, 1e7),
        name="forward",
    )(rows, w_in, w_out, *after)


def turned_kernel(me_ref, active_ref, rows_ref, *refs):
    pieces = refs[: 2 * NY]
    active_t_ref, rows_t_ref, next_ref, next_t_ref = refs[2 * NY :]
    active_t_ref[...] = active_ref[...].T

    @pl.when(pl.program_id(0) == 0)
    def _():
        rows_t_ref[...] = flat(rows_ref).T
        line_up(me_ref[1], pieces, next_ref)
        next_t_ref[...] = next_ref[...].T


def turned(me, active, rows, pieces, tile=512):
    slots, hid = active.shape
    width = rows.shape[2]
    piece = pl.BlockSpec(pieces[0].shape, lambda i: (0, 0))
    return pl.pallas_call(
        turned_kernel,
        grid=(hid // tile,),
        in_specs=[
            SMEM_SPEC,
            pl.BlockSpec((slots, tile), lambda i: (0, i)),
            rows_spec(rows.shape),
        ]
        + [piece] * len(pieces),
        out_specs=[
            pl.BlockSpec((tile, slots), lambda i: (i, 0)),
            pl.BlockSpec((width, slots), lambda i: (0, 0)),
            pl.BlockSpec((slots, width), lambda i: (0, 0)),
            pl.BlockSpec((width, slots), lambda i: (0, 0)),
        ],
        out_shape=[
            jax.ShapeDtypeStruct((hid, slots), BF16),
            jax.ShapeDtypeStruct((width, slots), BF16),
            jax.ShapeDtypeStruct((slots, width), BF16),
            jax.ShapeDtypeStruct((width, slots), BF16),
        ],
        compiler_params=params(58),
        cost_estimate=cost(5e9, 6e6),
        name="turned",
    )(me, active, rows, *pieces)


SUB = 256


def turn_kernel(
    turned_ref,
    next_ref,
    cot_ref,
    w_in_ref,
    w_out_ref,
    slope_ref,
    active_ref,
    dh_ref,
    theta_out_ref,
    slope_next_ref,
    active_next_ref,
    produced_ref,
    total,
):
    step = pl.program_id(0)

    cot = cot_ref[...]
    tile = w_in_ref.shape[1]
    part = 0.0
    for at in range(0, tile, SUB):
        cols = slice(at, at + SUB)
        w_out = w_out_ref[cols, :]
        dh = (dot(cot, w_out, 1, 1) * slope_ref[:, cols]).astype(BF16)
        dh_ref[:, cols] = dh
        grad_in = dot(turned_ref[...], dh)
        theta_in = after_one(w_in_ref[:, cols].astype(F32), grad_in).astype(BF16)
        grad_out = dot(active_ref[cols, :], cot)
        theta_out = after_one(w_out.astype(F32), grad_out).astype(BF16)
        theta_out_ref[cols, :] = theta_out
        active, slope_next_ref[:, cols] = gelu_and_slope(dot(next_ref[...], theta_in))
        active = active.astype(BF16)
        active_next_ref[:, cols] = active
        part += dot(active, theta_out)

    @pl.when(step == 0)
    def _():
        total[...] = part

    @pl.when(step > 0)
    def _():
        total[...] += part

    @pl.when(step == pl.num_programs(0) - 1)
    def _():
        produced_ref[...] = total[...].astype(BF16)


def turn(rows_t, next_rows, cot, w_in, w_out, slope, active_t, tile=512):
    slots, width = next_rows.shape
    hid = w_in.shape[1]
    whole = pl.BlockSpec((slots, width), lambda i: (0, 0))
    by_col = pl.BlockSpec((slots, tile), lambda i: (0, i))
    by_row = pl.BlockSpec((tile, width), lambda i: (i, 0))
    return pl.pallas_call(
        turn_kernel,
        grid=(hid // tile,),
        in_specs=[
            pl.BlockSpec((width, slots), lambda i: (0, 0)),
            whole,
            whole,
            pl.BlockSpec((width, tile), lambda i: (0, i)),
            by_row,
            by_col,
            pl.BlockSpec((tile, slots), lambda i: (i, 0)),
        ],
        out_specs=[by_col, by_row, by_col, by_col, whole],
        out_shape=[
            jax.ShapeDtypeStruct((slots, hid), BF16),
            jax.ShapeDtypeStruct((hid, width), BF16),
            jax.ShapeDtypeStruct((slots, hid), F32),
            jax.ShapeDtypeStruct((slots, hid), BF16),
            jax.ShapeDtypeStruct((slots, width), BF16),
        ],
        scratch_shapes=[pltpu.VMEM((slots, width), F32)],
        compiler_params=params(58),
        cost_estimate=cost(1.5e10, 2e7),
        name="turn",
    )(rows_t, next_rows, cot, w_in, w_out, slope, active_t)


PARTS = {
    0: (("own", 0), ("own", 2)),
    1: (("far_plus", 2), ("near_plus", 0)),
    2: (("far_minus", 0), ("far_plus", 0)),
    3: (("near_minus", 0), ("far_minus", 2)),
}
PART_SHARDS = {"far_minus": 4, "far_plus": 4, "near_minus": 2, "near_plus": 2, "own": 4}
HALVES = ((1, 3), (0, 2))


def store_band(k, m, change, outs):
    half = 0 if m in HALVES[0] else 1
    name, at = PARTS[k][half]
    outs[name][at + HALVES[half].index(m)] = change.astype(BF16)


def ahead_kernel(w_ref, active_t_ref, cot_ref, active_next_ref, grad_ref, part_ref, next_t_ref):
    grad = dot(active_t_ref[...], cot_ref[...])
    grad_ref[...] = grad
    part_ref[...] = first_part(w_ref[...].astype(F32), grad)
    next_t_ref[...] = active_next_ref[...].T


def ahead(w_out, active_t, cot, active_next, tile=384):
    hid, slots = active_t.shape
    width = cot.shape[1]
    by_row = pl.BlockSpec((tile, width), lambda i: (i, 0))
    by_slot = pl.BlockSpec((tile, slots), lambda i: (i, 0))
    return pl.pallas_call(
        ahead_kernel,
        grid=(hid // tile,),
        in_specs=[
            by_row,
            by_slot,
            pl.BlockSpec((slots, width), lambda i: (0, 0)),
            pl.BlockSpec((slots, tile), lambda i: (0, i)),
        ],
        out_specs=[by_row, by_row, by_slot],
        out_shape=[jax.ShapeDtypeStruct((hid, width), F32)] * 2
        + [jax.ShapeDtypeStruct((hid, slots), BF16)],
        compiler_params=params(58),
        cost_estimate=cost(7e9, 1.5e7),
        name="ahead",
    )(w_out, active_t, cot, active_next)


def change_out_kernel(rep_ref, grad_one, part_one, active_t, cot, *rest):
    outs = dict(zip(PART_SHARDS, rest[:5]))
    grad_two = rest[5]
    grad_two[...] = dot(active_t[...], cot[...])
    band = outs["own"].shape[1]
    x = rep_ref[0] % NX
    for m in range(NZ):

        @pl.when(pl.program_id(0) == m)
        def _():
            for k in range(NX):
                rows = pl.ds(pl.multiple_of((x + k) % NX * band, 16), band)
                change = part_one[rows, :] + second_part(grad_one[rows, :], grad_two[rows, :])
                store_band(k, m, change, outs)


def change_out(rep, replicas, grad_one, part_one, active_t, cot):
    hid, slots = active_t.shape
    width = cot.shape[1]
    band = hid // replicas
    tile = band * NX

    def z_of(i, rep_ref):
        return jnp.bitwise_xor(rep_ref[0] // NX, i)

    by_row = pl.BlockSpec((tile, width), lambda i, r: (z_of(i, r), 0))
    return pl.pallas_call(
        change_out_kernel,
        grid_spec=pltpu.PrefetchScalarGridSpec(
            num_scalar_prefetch=1,
            grid=(NZ,),
            in_specs=[
                by_row,
                by_row,
                pl.BlockSpec((tile, slots), lambda i, r: (z_of(i, r), 0)),
                pl.BlockSpec((slots, width), lambda i, r: (0, 0)),
            ],
            out_specs=[
                pl.BlockSpec((n, band, width), lambda i, r: (0, 0, 0)) for n in PART_SHARDS.values()
            ],
            scratch_shapes=[pltpu.VMEM((tile, width), F32)],
        ),
        out_shape=[jax.ShapeDtypeStruct((n, band, width), BF16) for n in PART_SHARDS.values()],
        compiler_params=params(),
        cost_estimate=cost(8e9, 1e7),
        name="change_out",
    )(rep, grad_one, part_one, active_t, cot)


def change_in_kernel(
    rep_ref, w_ref, one_t, dh_one, two_t, cot_two, theta_out, slope_two, *rest
):
    outs = dict(zip(PART_SHARDS, rest[:5]))
    grad_one, grad_two = rest[5:]
    upstream = dot(cot_two[...], theta_out[...], 1, 1)
    dh_two = (upstream * slope_two[...]).astype(BF16)
    grad_one[...] = dot(one_t[...], dh_one[...])
    grad_two[...] = dot(two_t[...], dh_two)
    band = outs["own"].shape[1]
    x, z = rep_ref[0] % NX, rep_ref[0] // NX
    for k in range(NX):
        for m in range(NZ):
            first = pl.multiple_of((jnp.bitwise_xor(z, m) * NX + (x + k) % NX) * band, 16)
            rows = pl.ds(first, band)
            change = change_of_two(w_ref[rows, :].astype(F32), grad_one[rows, :], grad_two[rows, :])
            store_band(k, m, change, outs)


def change_in(rep, replicas, one_t, two_t, w_in, dh_one, cot_two, theta_out, slope_two, tile=256):
    slots, hid = dh_one.shape
    width = one_t.shape[0]
    band = width // replicas
    whole = pl.BlockSpec((slots, width), lambda i: (0, 0))
    by_col = pl.BlockSpec((slots, tile), lambda i: (0, i))
    turned_spec = pl.BlockSpec((width, slots), lambda i: (0, 0))
    return pl.pallas_call(
        change_in_kernel,
        grid=(hid // tile,),
        in_specs=[
            SMEM_SPEC,
            pl.BlockSpec((width, tile), lambda i: (0, i)),
            turned_spec,
            by_col,
            turned_spec,
            whole,
            pl.BlockSpec((tile, width), lambda i: (i, 0)),
            by_col,
        ],
        out_specs=[pl.BlockSpec((n, band, tile), lambda i: (0, 0, i)) for n in PART_SHARDS.values()],
        out_shape=[jax.ShapeDtypeStruct((n, band, hid), BF16) for n in PART_SHARDS.values()],
        scratch_shapes=[
            pltpu.VMEM((width, tile), F32),
            pltpu.VMEM((width, tile), F32),
        ],
        compiler_params=params(48),
        cost_estimate=cost(1.2e10, 1.5e7),
        name="change_in",
    )(rep, w_in, one_t, dh_one, two_t, cot_two, theta_out, slope_two)


def rep_permutation(step_x, flip_z):
    pairs = []
    for z in range(NZ):
        for x in range(NX):
            pairs.append((z * NX + x, (z ^ flip_z) * NX + (x + step_x) % NX))
    return pairs


def shift_x(array, step):
    return lax.ppermute(array, "rep", rep_permutation(step, 0))


def swap_z(array, flip):
    return lax.ppermute(array, "rep", rep_permutation(0, flip))


def near_kernel(near_minus, near_plus, from_plus, from_minus, *refs):
    to_minus, to_plus = refs[-2:]
    to_minus[...] = (near_minus[...].astype(F32) + from_plus[:2].astype(F32)).astype(BF16)
    to_plus[...] = (near_plus[...].astype(F32) + from_minus[:2].astype(F32)).astype(BF16)


def sum_kernel(held, own, from_plus, from_minus, last_plus, last_minus, *refs):
    outs = refs[2 * held :]
    for half, members in enumerate(HALVES):
        for i, m in enumerate(members):
            total = own[2 * half + i].astype(F32)
            if half == 0:
                total += from_minus[2 + i].astype(F32) + last_plus[i].astype(F32)
            else:
                total += from_plus[2 + i].astype(F32) + last_minus[i].astype(F32)
            outs[m][...] = total.astype(outs[m].dtype)


def start_far(parts):
    return shift_x(parts[0], -1), shift_x(parts[1], 1)


def near_sums(parts, far, after):
    return small_call(
        near_kernel,
        [jax.ShapeDtypeStruct(parts[2].shape, BF16)] * 2,
        "near",
        [VMEM_SPEC] * 4 + [ANY_SPEC] * len(after),
        parts[2],
        parts[3],
        *far,
        *after,
    )


def owner_terms(parts, far, near, held):
    band_shape = parts[4].shape[1:]
    last = shift_x(near[0], -1), shift_x(near[1], 1)
    out = pl.pallas_call(
        functools.partial(sum_kernel, len(held)),
        in_specs=[VMEM_SPEC] * 5 + [ANY_SPEC] * len(held),
        out_specs=[ANY_SPEC] * len(held) + [VMEM_SPEC] * NZ,
        out_shape=[jax.ShapeDtypeStruct(a.shape, BF16) for a in held]
        + [jax.ShapeDtypeStruct(band_shape, F32 if m == 0 else BF16) for m in range(NZ)],
        input_output_aliases={5 + i: i for i in range(len(held))},
        compiler_params=params(),
        cost_estimate=cost(1e3, 1e3),
        name="sums",
    )(parts[4], *far, *last, *held)
    return out[len(held) :], out[: len(held)]


def reduce_z(terms):
    return [terms[0]] + [swap_z(terms[m], m) for m in range(1, NZ)]


def update_kernel(replicas, me_ref, w_ref, mom_ref, *refs):
    new_w, new_mom = refs[NZ:]
    summed = refs[0][...]
    for term in refs[1:NZ]:
        summed += term[...].astype(F32)
    averaged = summed * (1.0 / replicas)
    momentum = 0.9 * mom_ref[...] + averaged
    new_mom[...] = momentum
    new_w[...] = (w_ref[...].astype(F32) - 0.7 * (averaged + 0.9 * momentum)).astype(BF16)


def outer_update(rep, replicas, w, momentum, terms):
    band, columns = momentum.shape
    whole = pl.BlockSpec((band, columns), lambda i, r: (0, 0))
    return pl.pallas_call(
        functools.partial(update_kernel, replicas),
        grid_spec=pltpu.PrefetchScalarGridSpec(
            num_scalar_prefetch=1,
            grid=(1,),
            in_specs=[pl.BlockSpec((band, columns), lambda i, r: (r[0], 0))] + [whole] * (1 + NZ),
            out_specs=[whole] * 2,
        ),
        out_shape=[
            jax.ShapeDtypeStruct((band, columns), BF16),
            jax.ShapeDtypeStruct((band, columns), F32),
        ],
        compiler_params=params(),
        cost_estimate=cost(1e3, 1e3),
        name="update",
    )(rep, w, momentum, *terms)


def stack_kernel(one, two, three, four, low, high):
    low[0], low[1], high[0], high[1] = one[...], two[...], three[...], four[...]


def assemble_kernel(rep_ref, *refs):
    out = refs[-1]
    x, z = rep_ref[0] % NX, rep_ref[0] // NX
    band = refs[0].shape[1]
    for k in range(NX):
        for m in range(NZ):
            first = pl.multiple_of((jnp.bitwise_xor(z, m) * NX + (x + k) % NX) * band, 16)
            out[pl.ds(first, band), :] = refs[2 * k + m // 2][m % 2]


def gather_from_owner(rep, own):
    band, columns = own.shape
    beside, across = swap_z(own, 1), swap_z(own, 2)
    others = [beside, across, swap_z(across, 1)]
    low, high = small_call(
        stack_kernel,
        [jax.ShapeDtypeStruct((2, band, columns), BF16)] * 2,
        "stack",
        [VMEM_SPEC] * NZ,
        own,
        *others,
    )
    low_minus, high_plus = shift_x(low, 1), shift_x(high, -1)
    high_minus, low_plus = shift_x(high, 1), shift_x(low, -1)
    low_cross, high_cross = shift_x(low_minus, 1), shift_x(high_plus, -1)
    tile = 384
    part = pl.BlockSpec((2, band, tile), lambda i: (0, 0, i))
    rows = NZ * NX * band
    return pl.pallas_call(
        assemble_kernel,
        grid=(columns // tile,),
        in_specs=[SMEM_SPEC] + [part] * 8,
        out_specs=pl.BlockSpec((rows, tile), lambda i: (0, i)),
        out_shape=jax.ShapeDtypeStruct((rows, columns), BF16),
        compiler_params=params(),
        cost_estimate=cost(1e3, 1e3),
        name="assemble",
    )(rep, low, high, low_plus, high_plus, low_cross, high_cross, low_minus, high_minus)


def exchange(rows, experts):
    slots, width = rows.shape
    block = rows.reshape(experts, slots // experts, width)
    return lax.all_to_all(block, "exp", split_axis=0, concat_axis=0, tiled=True).reshape(slots, width)


def per_device(w_in, w_out, mom_in, mom_out, frames, targets, routes, gates):
    experts = lax.axis_size("exp")
    replicas = lax.axis_size("rep")
    rep = lax.axis_index("rep")
    me = jnp.stack([rep, lax.axis_index("exp")]).astype(jnp.int32)
    capacity = 4 * frames.shape[2] // experts
    w_in, w_out, mom_in, mom_out = w_in[0], w_out[0], mom_in[0], mom_out[0]
    frames, targets, routes, gates = frames[0], targets[0], routes[0], gates[0]

    rows = lax.all_to_all(
        place_frames(routes[0], frames[0], experts, capacity),
        "exp",
        split_axis=0,
        concat_axis=0,
        tiled=True,
    )
    mine = jnp.zeros((8, frames.shape[1]), F32).at[:2].set(routes[1].T.astype(F32)), frames[1]
    mine = hold(mine, [rows])
    cross = [over_exp(array, flip_z=1) for array in mine]
    slope_one, active_one, produced = forward(rows, w_in, w_out, mine)
    (produced,) = hold([produced], cross)
    pieces = dispatch(capacity, me, *mine, *cross)
    returned = exchange(produced, experts)
    cot_one = exchange(place_residue(routes[0], gates[0], targets[0], returned, capacity, pieces), experts)
    active_t, one_t, rows_two, two_t = turned(me, active_one, rows, pieces)
    dh_one, theta_out, slope_two, active_two, produced = turn(
        one_t, rows_two, cot_one, w_in, w_out, slope_one, active_t
    )
    grad_one, part_one, active_t = ahead(w_out, active_t, cot_one, active_two)
    returned = exchange(produced, experts)
    cot_two = exchange(place_residue(routes[1], gates[1], targets[1], returned, capacity), experts)

    parts_out = change_out(me, replicas, grad_one, part_one, active_t, cot_two)
    far_out = start_far(parts_out)
    parts_in = change_in(
        me, replicas, one_t, two_t, w_in, dh_one, cot_two, theta_out, slope_two
    )
    near_out = near_sums(parts_out, far_out, parts_in[4:])
    terms_out, held = owner_terms(parts_out, far_out, near_out, parts_in[:2])
    parts_in = [*held, *parts_in[2:]]
    far_in = start_far(parts_in)
    terms_out = reduce_z(terms_out)
    near_in = near_sums(parts_in, far_in, parts_in[4:])
    terms_in = reduce_z(owner_terms(parts_in, far_in, near_in, [])[0])
    part_out, new_mom_out = outer_update(me, replicas, w_out, mom_out, terms_out)
    new_w_out = gather_from_owner(me, part_out)
    part_in, new_mom_in = outer_update(me, replicas, w_in, mom_in, terms_in)
    new_w_in = gather_from_owner(me, part_in)
    return (new_w_in[None], new_w_out[None], new_mom_in[None], new_mom_out[None])


def solution(mesh):
    in_specs = (
        P("exp", None, None),
        P("exp", None, None),
        P("exp", "rep", None),
        P("exp", "rep", None),
        P("rep", None, "exp", None),
        P("rep", None, "exp", None),
        P("rep", None, "exp", None),
        P("rep", None, "exp", None),
    )
    out_specs = (
        P("exp", None, None),
        P("exp", None, None),
        P("exp", "rep", None),
        P("exp", "rep", None),
    )
    return jax.shard_map(
        per_device, mesh=mesh, in_specs=in_specs, out_specs=out_specs, check_vma=False
    )
```

```python
import functools
import math

import jax
import jax.numpy as jnp
from jax import lax
from jax.experimental import pallas as pl
from jax.experimental.pallas import tpu as pltpu
from jax.sharding import PartitionSpec as P

F32 = jnp.float32
BF16 = jnp.bfloat16
MIB = 1 << 20
NX = 4
NZ = 4
NY = 4


SMEM_SPEC = pl.BlockSpec(memory_space=pltpu.SMEM)
VMEM_SPEC = pl.BlockSpec(memory_space=pltpu.VMEM)
ANY_SPEC = pl.BlockSpec(memory_space=pl.ANY)


def dot(left, right, on_left=1, on_right=0):
    return lax.dot_general(
        left, right, (((on_left,), (on_right,)), ((), ())), preferred_element_type=F32
    )


def slots_of(first, second):
    rows = first.shape[0]
    lane = lax.broadcasted_iota(jnp.int32, (rows, 128), 1)
    names_first, names_second = lane == first, lane == second
    named = jnp.where(names_first | names_second, 1.0, 0.0).astype(BF16)
    earlier = lax.broadcasted_iota(jnp.int32, (rows, rows), 0) > lax.broadcasted_iota(
        jnp.int32, (rows, rows), 1
    )
    count = dot(jnp.where(earlier, 1.0, 0.0).astype(BF16), named)
    slot_first = jnp.sum(jnp.where(names_first, count, 0.0), axis=1, keepdims=True)
    slot_second = jnp.sum(jnp.where(names_second, count, 0.0), axis=1, keepdims=True)
    return slot_first.astype(jnp.int32), slot_second.astype(jnp.int32)


def places(routes, capacity):
    first, second = routes[:, 0:1], routes[:, 1:2]
    slot_first, slot_second = slots_of(first, second)
    return first * capacity + slot_first, second * capacity + slot_second


def one_hot(place, size):
    lane = lax.broadcasted_iota(jnp.int32, (place.shape[0], size), 1)
    return jnp.where(lane == place, 1.0, 0.0).astype(BF16)


def gelu_and_slope(x):
    c = math.sqrt(2.0 / math.pi)
    square = x * x
    bent = jnp.tanh(c * (x + 0.044715 * (square * x)))
    half = 0.5 * (1.0 + bent)
    slope = half + 0.5 * x * (1.0 - bent * bent) * (c * (1.0 + 3 * 0.044715 * square))
    return x * half, slope


RATE, DECAY = 0.004, 0.1
KEEP = 1.0 - RATE * DECAY


def inverse(x):
    near = pl.reciprocal(x, approx=True)
    return near * (2.0 - x * near)


def after_one(weight, grad):
    return KEEP * weight - RATE * (grad * inverse(jnp.abs(grad) + 0.01))


def first_part(weight, grad_one):
    ratio = grad_one * inverse(jnp.abs(grad_one) + 0.01)
    return (1.0 - KEEP * KEEP) * weight + (RATE * KEEP) * ratio


def second_part(grad_one, grad_two):
    first = (0.09 / 0.19) * grad_one + (0.1 / 0.19) * grad_two
    second = (0.0475 / 0.0975) * (grad_one * grad_one) + (0.05 / 0.0975) * (grad_two * grad_two)
    return RATE * (first * inverse(second * lax.rsqrt(second + 1e-30) + 0.01))


def change_of_two(weight, grad_one, grad_two):
    first = (0.09 / 0.19) * grad_one + (0.1 / 0.19) * grad_two
    second = (0.0475 / 0.0975) * (grad_one * grad_one) + (0.05 / 0.0975) * (grad_two * grad_two)
    below_two = second * lax.rsqrt(second + 1e-30) + 0.01
    below_one = jnp.abs(grad_one) + 0.01
    over = KEEP * (grad_one * below_two) + first * below_one
    return (1.0 - KEEP * KEEP) * weight + RATE * (over * inverse(below_one * below_two))


def params(limit=48):
    return pltpu.CompilerParams(vmem_limit_bytes=limit * MIB)


def cost(flops, size):
    return pl.CostEstimate(flops=int(flops), bytes_accessed=int(size), transcendentals=0)


def small_call(kernel, out_shape, name, in_specs, *operands, **more):
    return pl.pallas_call(
        kernel,
        in_specs=in_specs,
        out_specs=jax.tree.map(lambda _: VMEM_SPEC, out_shape),
        out_shape=out_shape,
        compiler_params=params(),
        cost_estimate=cost(1e3, 1e3),
        name=name,
        **more,
    )(*operands)


def place_kernel(capacity, routes_ref, frames_ref, out_ref):
    experts, _, width = out_ref.shape
    size = experts * capacity
    first, second = places(routes_ref[...], capacity)
    spread = one_hot(first, size) + one_hot(second, size)
    placed = dot(spread, frames_ref[0], 0, 0).astype(BF16)
    out_ref[...] = placed.reshape(experts, capacity, width)


def place_frames(routes, frames, experts, capacity):
    return pl.pallas_call(
        functools.partial(place_kernel, capacity),
        grid=(1,),
        in_specs=[
            pl.BlockSpec(routes.shape, lambda i: (0, 0)),
            pl.BlockSpec((1, *frames.shape[1:]), lambda i: (0, 0, 0)),
        ],
        out_specs=pl.BlockSpec((experts, capacity, frames.shape[2]), lambda i: (0, 0, 0)),
        out_shape=jax.ShapeDtypeStruct((experts, capacity, frames.shape[2]), BF16),
        compiler_params=params(),
        cost_estimate=cost(2e9, 3e6),
        name="place_frames",
    )(routes, frames)


def spread_kernel(capacity, me_ref, routes_a, a_ref, routes_b, b_ref, *outs):
    me = me_ref[1]
    for block, (routes_ref, rows_ref) in enumerate(((routes_a, a_ref), (routes_b, b_ref))):
        routes = routes_ref[...].T.astype(jnp.int32)
        pair = routes[:, 0:1], routes[:, 1:2]
        hot = 0.0
        for expert, slot in zip(pair, slots_of(*pair)):
            ahead = jnp.bitwise_and((expert >> 2) - (me >> 2), NY - 1)
            here = jnp.bitwise_and(expert, 3) == jnp.bitwise_and(me, 3)
            hot += one_hot(jnp.where(here, ahead * capacity + slot, -1), NY * capacity)
        placed = dot(hot, rows_ref[...], 0, 0).astype(BF16)
        for ahead, out in enumerate(outs):
            out[block * capacity : (block + 1) * capacity, :] = placed[
                ahead * capacity : (ahead + 1) * capacity
            ]


def spread_rows(capacity, me, *blocks):
    width = blocks[1].shape[1]
    return small_call(
        functools.partial(spread_kernel, capacity),
        [jax.ShapeDtypeStruct((2 * capacity, width), BF16)] * NY,
        "spread_rows",
        [SMEM_SPEC] + [VMEM_SPEC] * 4,
        me,
        *blocks,
    )


def over_exp(array, along_y=0, flip_z=0, flip_core=0):
    pairs = []
    for y in range(NY):
        for z in range(2):
            for core in range(2):
                target = ((y + along_y) % NY, z ^ flip_z, core ^ flip_core)
                pairs.append((y * 4 + z * 2 + core, target[0] * 4 + target[1] * 2 + target[2]))
    return lax.ppermute(array, "exp", pairs)


def hold(arrays, after):
    return pl.pallas_call(
        lambda *refs: None,
        in_specs=[ANY_SPEC] * (len(arrays) + len(after)),
        out_specs=[ANY_SPEC] * len(arrays),
        out_shape=[jax.ShapeDtypeStruct(a.shape, a.dtype) for a in arrays],
        input_output_aliases={i: i for i in range(len(arrays))},
        cost_estimate=cost(1e3, 1e3),
        name="hold",
    )(*arrays, *after)


def dispatch(capacity, me, routes, own, cross_routes, cross):
    near = spread_rows(
        capacity, me, routes, own, over_exp(routes, flip_core=1), over_exp(own, flip_core=1)
    )
    far = spread_rows(
        capacity,
        me,
        cross_routes,
        cross,
        over_exp(cross_routes, flip_core=1),
        over_exp(cross, flip_core=1),
    )
    return [
        over_exp(piece, along_y=i) if i else piece for side in (near, far) for i, piece in enumerate(side)
    ]


def line_up(me, pieces, out):
    capacity = pieces[0].shape[0] // 2
    for at, piece in enumerate(pieces):
        for block in range(2):
            y = jnp.bitwise_and((me >> 2) - at % NY, NY - 1)
            place_of = jnp.bitwise_xor(jnp.bitwise_and(me, 3), 2 * (at // NY) + block)
            first = pl.multiple_of((y * 4 + place_of) * capacity, 32)
            out[pl.ds(first, capacity), :] = piece[block * capacity : (block + 1) * capacity, :]


def residue_kernel(capacity, routes_ref, gates_ref, targets_ref, returned_ref, *refs):
    out_ref = refs[-1]
    size = out_ref.shape[0]
    rows = routes_ref.shape[0]
    first, second = places(routes_ref[...], capacity)
    hot_first, hot_second = one_hot(first, size), one_hot(second, size)
    gate_first, gate_second = gates_ref[:, 0:1], gates_ref[:, 1:2]
    returned = returned_ref[...]
    combined = gate_first * dot(hot_first, returned) + gate_second * dot(hot_second, returned)
    residue = (combined - targets_ref[...].astype(F32)) * (1.0 / rows)
    cot_first = (gate_first * residue).astype(BF16)
    cot_second = (gate_second * residue).astype(BF16)
    out_ref[...] = (dot(hot_first, cot_first, 0, 0) + dot(hot_second, cot_second, 0, 0)).astype(BF16)


def place_residue(routes, gates, targets, returned, capacity, after=()):
    return small_call(
        functools.partial(residue_kernel, capacity),
        jax.ShapeDtypeStruct(returned.shape, BF16),
        "place_residue",
        [VMEM_SPEC] * 4 + [ANY_SPEC] * len(after),
        routes,
        gates,
        targets,
        returned,
        *after,
    )


def flat(ref):
    return ref[...].reshape(-1, ref.shape[-1])


def rows_spec(shape):
    return pl.BlockSpec(shape, lambda i: (0, 0, 0))


def forward_kernel(rows_ref, w_in_ref, w_out_ref, *refs):
    slope_ref, active_ref, produced_ref, total = refs[-4:]
    step = pl.program_id(0)
    active, slope_ref[...] = gelu_and_slope(dot(flat(rows_ref), w_in_ref[...]))
    active = active.astype(BF16)
    active_ref[...] = active
    part = dot(active, w_out_ref[...])

    @pl.when(step == 0)
    def _():
        total[...] = part

    @pl.when(step > 0)
    def _():
        total[...] += part

    @pl.when(step == pl.num_programs(0) - 1)
    def _():
        produced_ref[...] = total[...].astype(BF16)


def forward(rows, w_in, w_out, after, tile=512):
    experts, capacity, width = rows.shape
    slots = experts * capacity
    hid = w_in.shape[1]
    whole = pl.BlockSpec((slots, width), lambda i: (0, 0))
    by_col = pl.BlockSpec((slots, tile), lambda i: (0, i))
    return pl.pallas_call(
        forward_kernel,
        grid=(hid // tile,),
        in_specs=[
            rows_spec(rows.shape),
            pl.BlockSpec((width, tile), lambda i: (0, i)),
            pl.BlockSpec((tile, width), lambda i: (i, 0)),
        ]
        + [ANY_SPEC] * len(after),
        out_specs=[by_col, by_col, whole],
        out_shape=[
            jax.ShapeDtypeStruct((slots, hid), F32),
            jax.ShapeDtypeStruct((slots, hid), BF16),
            jax.ShapeDtypeStruct((slots, width), BF16),
        ],
        scratch_shapes=[pltpu.VMEM((slots, width), F32)],
        compiler_params=params(58),
        cost_estimate=cost(7e9, 1e7),
        name="forward",
    )(rows, w_in, w_out, *after)


def turned_kernel(me_ref, active_ref, rows_ref, *refs):
    pieces = refs[: 2 * NY]
    active_t_ref, rows_t_ref, next_ref, next_t_ref = refs[2 * NY :]
    active_t_ref[...] = active_ref[...].T

    @pl.when(pl.program_id(0) == 0)
    def _():
        rows_t_ref[...] = flat(rows_ref).T
        line_up(me_ref[1], pieces, next_ref)
        next_t_ref[...] = next_ref[...].T


def turned(me, active, rows, pieces, tile=512):
    slots, hid = active.shape
    width = rows.shape[2]
    piece = pl.BlockSpec(pieces[0].shape, lambda i: (0, 0))
    return pl.pallas_call(
        turned_kernel,
        grid=(hid // tile,),
        in_specs=[
            SMEM_SPEC,
            pl.BlockSpec((slots, tile), lambda i: (0, i)),
            rows_spec(rows.shape),
        ]
        + [piece] * len(pieces),
        out_specs=[
            pl.BlockSpec((tile, slots), lambda i: (i, 0)),
            pl.BlockSpec((width, slots), lambda i: (0, 0)),
            pl.BlockSpec((slots, width), lambda i: (0, 0)),
            pl.BlockSpec((width, slots), lambda i: (0, 0)),
        ],
        out_shape=[
            jax.ShapeDtypeStruct((hid, slots), BF16),
            jax.ShapeDtypeStruct((width, slots), BF16),
            jax.ShapeDtypeStruct((slots, width), BF16),
            jax.ShapeDtypeStruct((width, slots), BF16),
        ],
        compiler_params=params(58),
        cost_estimate=cost(5e9, 6e6),
        name="turned",
    )(me, active, rows, *pieces)


SUB = 256


def turn_kernel(
    turned_ref,
    next_ref,
    cot_ref,
    w_in_ref,
    w_out_ref,
    slope_ref,
    active_ref,
    dh_ref,
    theta_out_ref,
    slope_next_ref,
    active_next_ref,
    produced_ref,
    total,
):
    step = pl.program_id(0)

    cot = cot_ref[...]
    tile = w_in_ref.shape[1]
    part = 0.0
    for at in range(0, tile, SUB):
        cols = slice(at, at + SUB)
        w_out = w_out_ref[cols, :]
        dh = (dot(cot, w_out, 1, 1) * slope_ref[:, cols]).astype(BF16)
        dh_ref[:, cols] = dh
        grad_in = dot(turned_ref[...], dh)
        theta_in = after_one(w_in_ref[:, cols].astype(F32), grad_in).astype(BF16)
        grad_out = dot(active_ref[cols, :], cot)
        theta_out = after_one(w_out.astype(F32), grad_out).astype(BF16)
        theta_out_ref[cols, :] = theta_out
        active, slope_next_ref[:, cols] = gelu_and_slope(dot(next_ref[...], theta_in))
        active = active.astype(BF16)
        active_next_ref[:, cols] = active
        part += dot(active, theta_out)

    @pl.when(step == 0)
    def _():
        total[...] = part

    @pl.when(step > 0)
    def _():
        total[...] += part

    @pl.when(step == pl.num_programs(0) - 1)
    def _():
        produced_ref[...] = total[...].astype(BF16)


def turn(rows_t, next_rows, cot, w_in, w_out, slope, active_t, tile=512):
    slots, width = next_rows.shape
    hid = w_in.shape[1]
    whole = pl.BlockSpec((slots, width), lambda i: (0, 0))
    by_col = pl.BlockSpec((slots, tile), lambda i: (0, i))
    by_row = pl.BlockSpec((tile, width), lambda i: (i, 0))
    return pl.pallas_call(
        turn_kernel,
        grid=(hid // tile,),
        in_specs=[
            pl.BlockSpec((width, slots), lambda i: (0, 0)),
            whole,
            whole,
            pl.BlockSpec((width, tile), lambda i: (0, i)),
            by_row,
            by_col,
            pl.BlockSpec((tile, slots), lambda i: (i, 0)),
        ],
        out_specs=[by_col, by_row, by_col, by_col, whole],
        out_shape=[
            jax.ShapeDtypeStruct((slots, hid), BF16),
            jax.ShapeDtypeStruct((hid, width), BF16),
            jax.ShapeDtypeStruct((slots, hid), F32),
            jax.ShapeDtypeStruct((slots, hid), BF16),
            jax.ShapeDtypeStruct((slots, width), BF16),
        ],
        scratch_shapes=[pltpu.VMEM((slots, width), F32)],
        compiler_params=params(58),
        cost_estimate=cost(1.5e10, 2e7),
        name="turn",
    )(rows_t, next_rows, cot, w_in, w_out, slope, active_t)


PARTS = {
    0: (("own", 0), ("own", 2)),
    1: (("far_plus", 2), ("near_plus", 0)),
    2: (("far_minus", 0), ("far_plus", 0)),
    3: (("near_minus", 0), ("far_minus", 2)),
}
PART_SHARDS = {"far_minus": 4, "far_plus": 4, "near_minus": 2, "near_plus": 2, "own": 4}
HALVES = ((1, 3), (0, 2))


def store_band(k, m, change, outs):
    half = 0 if m in HALVES[0] else 1
    name, at = PARTS[k][half]
    outs[name][at + HALVES[half].index(m)] = change.astype(BF16)


def ahead_kernel(w_ref, active_t_ref, cot_ref, active_next_ref, grad_ref, part_ref, next_t_ref):
    grad = dot(active_t_ref[...], cot_ref[...])
    grad_ref[...] = grad
    part_ref[...] = first_part(w_ref[...].astype(F32), grad)
    next_t_ref[...] = active_next_ref[...].T


def ahead(w_out, active_t, cot, active_next, tile=384):
    hid, slots = active_t.shape
    width = cot.shape[1]
    by_row = pl.BlockSpec((tile, width), lambda i: (i, 0))
    by_slot = pl.BlockSpec((tile, slots), lambda i: (i, 0))
    return pl.pallas_call(
        ahead_kernel,
        grid=(hid // tile,),
        in_specs=[
            by_row,
            by_slot,
            pl.BlockSpec((slots, width), lambda i: (0, 0)),
            pl.BlockSpec((slots, tile), lambda i: (0, i)),
        ],
        out_specs=[by_row, by_row, by_slot],
        out_shape=[jax.ShapeDtypeStruct((hid, width), F32)] * 2
        + [jax.ShapeDtypeStruct((hid, slots), BF16)],
        compiler_params=params(58),
        cost_estimate=cost(7e9, 1.5e7),
        name="ahead",
    )(w_out, active_t, cot, active_next)


def change_out_kernel(rep_ref, grad_one, part_one, active_t, cot, *rest):
    outs = dict(zip(PART_SHARDS, rest[:5]))
    grad_two = rest[5]
    grad_two[...] = dot(active_t[...], cot[...])
    band = outs["own"].shape[1]
    x = rep_ref[0] % NX
    for m in range(NZ):

        @pl.when(pl.program_id(0) == m)
        def _():
            for k in range(NX):
                rows = pl.ds(pl.multiple_of((x + k) % NX * band, 16), band)
                change = part_one[rows, :] + second_part(grad_one[rows, :], grad_two[rows, :])
                store_band(k, m, change, outs)


def change_out(rep, replicas, grad_one, part_one, active_t, cot):
    hid, slots = active_t.shape
    width = cot.shape[1]
    band = hid // replicas
    tile = band * NX

    def z_of(i, rep_ref):
        return jnp.bitwise_xor(rep_ref[0] // NX, i)

    by_row = pl.BlockSpec((tile, width), lambda i, r: (z_of(i, r), 0))
    return pl.pallas_call(
        change_out_kernel,
        grid_spec=pltpu.PrefetchScalarGridSpec(
            num_scalar_prefetch=1,
            grid=(NZ,),
            in_specs=[
                by_row,
                by_row,
                pl.BlockSpec((tile, slots), lambda i, r: (z_of(i, r), 0)),
                pl.BlockSpec((slots, width), lambda i, r: (0, 0)),
            ],
            out_specs=[
                pl.BlockSpec((n, band, width), lambda i, r: (0, 0, 0)) for n in PART_SHARDS.values()
            ],
            scratch_shapes=[pltpu.VMEM((tile, width), F32)],
        ),
        out_shape=[jax.ShapeDtypeStruct((n, band, width), BF16) for n in PART_SHARDS.values()],
        compiler_params=params(),
        cost_estimate=cost(8e9, 1e7),
        name="change_out",
    )(rep, grad_one, part_one, active_t, cot)


def change_in_kernel(
    rep_ref, w_ref, one_t, dh_one, two_t, cot_two, theta_out, slope_two, *rest
):
    outs = dict(zip(PART_SHARDS, rest[:5]))
    grad_one, grad_two = rest[5:]
    upstream = dot(cot_two[...], theta_out[...], 1, 1)
    dh_two = (upstream * slope_two[...]).astype(BF16)
    grad_one[...] = dot(one_t[...], dh_one[...])
    grad_two[...] = dot(two_t[...], dh_two)
    band = outs["own"].shape[1]
    x, z = rep_ref[0] % NX, rep_ref[0] // NX
    for k in range(NX):
        for m in range(NZ):
            first = pl.multiple_of((jnp.bitwise_xor(z, m) * NX + (x + k) % NX) * band, 16)
            rows = pl.ds(first, band)
            change = change_of_two(w_ref[rows, :].astype(F32), grad_one[rows, :], grad_two[rows, :])
            store_band(k, m, change, outs)


def change_in(rep, replicas, one_t, two_t, w_in, dh_one, cot_two, theta_out, slope_two, tile=256):
    slots, hid = dh_one.shape
    width = one_t.shape[0]
    band = width // replicas
    whole = pl.BlockSpec((slots, width), lambda i: (0, 0))
    by_col = pl.BlockSpec((slots, tile), lambda i: (0, i))
    turned_spec = pl.BlockSpec((width, slots), lambda i: (0, 0))
    return pl.pallas_call(
        change_in_kernel,
        grid=(hid // tile,),
        in_specs=[
            SMEM_SPEC,
            pl.BlockSpec((width, tile), lambda i: (0, i)),
            turned_spec,
            by_col,
            turned_spec,
            whole,
            pl.BlockSpec((tile, width), lambda i: (i, 0)),
            by_col,
        ],
        out_specs=[pl.BlockSpec((n, band, tile), lambda i: (0, 0, i)) for n in PART_SHARDS.values()],
        out_shape=[jax.ShapeDtypeStruct((n, band, hid), BF16) for n in PART_SHARDS.values()],
        scratch_shapes=[
            pltpu.VMEM((width, tile), F32),
            pltpu.VMEM((width, tile), F32),
        ],
        compiler_params=params(48),
        cost_estimate=cost(1.2e10, 1.5e7),
        name="change_in",
    )(rep, w_in, one_t, dh_one, two_t, cot_two, theta_out, slope_two)


def rep_permutation(step_x, flip_z):
    pairs = []
    for z in range(NZ):
        for x in range(NX):
            pairs.append((z * NX + x, (z ^ flip_z) * NX + (x + step_x) % NX))
    return pairs


def shift_x(array, step):
    return lax.ppermute(array, "rep", rep_permutation(step, 0))


def swap_z(array, flip):
    return lax.ppermute(array, "rep", rep_permutation(0, flip))


def near_kernel(near_minus, near_plus, from_plus, from_minus, *refs):
    to_minus, to_plus = refs[-2:]
    to_minus[...] = (near_minus[...].astype(F32) + from_plus[:2].astype(F32)).astype(BF16)
    to_plus[...] = (near_plus[...].astype(F32) + from_minus[:2].astype(F32)).astype(BF16)


def sum_kernel(held, own, from_plus, from_minus, last_plus, last_minus, *refs):
    outs = refs[2 * held :]
    for half, members in enumerate(HALVES):
        for i, m in enumerate(members):
            total = own[2 * half + i].astype(F32)
            if half == 0:
                total += from_minus[2 + i].astype(F32) + last_plus[i].astype(F32)
            else:
                total += from_plus[2 + i].astype(F32) + last_minus[i].astype(F32)
            outs[m][...] = total.astype(outs[m].dtype)


def start_far(parts):
    return shift_x(parts[0], -1), shift_x(parts[1], 1)


def near_sums(parts, far, after):
    return small_call(
        near_kernel,
        [jax.ShapeDtypeStruct(parts[2].shape, BF16)] * 2,
        "near",
        [VMEM_SPEC] * 4 + [ANY_SPEC] * len(after),
        parts[2],
        parts[3],
        *far,
        *after,
    )


def owner_terms(parts, far, near, held):
    band_shape = parts[4].shape[1:]
    last = shift_x(near[0], -1), shift_x(near[1], 1)
    out = pl.pallas_call(
        functools.partial(sum_kernel, len(held)),
        in_specs=[VMEM_SPEC] * 5 + [ANY_SPEC] * len(held),
        out_specs=[ANY_SPEC] * len(held) + [VMEM_SPEC] * NZ,
        out_shape=[jax.ShapeDtypeStruct(a.shape, BF16) for a in held]
        + [jax.ShapeDtypeStruct(band_shape, F32 if m == 0 else BF16) for m in range(NZ)],
        input_output_aliases={5 + i: i for i in range(len(held))},
        compiler_params=params(),
        cost_estimate=cost(1e3, 1e3),
        name="sums",
    )(parts[4], *far, *last, *held)
    return out[len(held) :], out[: len(held)]


def reduce_z(terms):
    return [terms[0]] + [swap_z(terms[m], m) for m in range(1, NZ)]


def update_kernel(replicas, me_ref, w_ref, mom_ref, *refs):
    new_w, new_mom = refs[NZ:]
    summed = refs[0][...]
    for term in refs[1:NZ]:
        summed += term[...].astype(F32)
    averaged = summed * (1.0 / replicas)
    momentum = 0.9 * mom_ref[...] + averaged
    new_mom[...] = momentum
    new_w[...] = (w_ref[...].astype(F32) - 0.7 * (averaged + 0.9 * momentum)).astype(BF16)


def outer_update(rep, replicas, w, momentum, terms):
    band, columns = momentum.shape
    whole = pl.BlockSpec((band, columns), lambda i, r: (0, 0))
    return pl.pallas_call(
        functools.partial(update_kernel, replicas),
        grid_spec=pltpu.PrefetchScalarGridSpec(
            num_scalar_prefetch=1,
            grid=(1,),
            in_specs=[pl.BlockSpec((band, columns), lambda i, r: (r[0], 0))] + [whole] * (1 + NZ),
            out_specs=[whole] * 2,
        ),
        out_shape=[
            jax.ShapeDtypeStruct((band, columns), BF16),
            jax.ShapeDtypeStruct((band, columns), F32),
        ],
        compiler_params=params(),
        cost_estimate=cost(1e3, 1e3),
        name="update",
    )(rep, w, momentum, *terms)


def stack_kernel(one, two, three, four, low, high):
    low[0], low[1], high[0], high[1] = one[...], two[...], three[...], four[...]


def assemble_kernel(rep_ref, *refs):
    out = refs[-1]
    x, z = rep_ref[0] % NX, rep_ref[0] // NX
    band = refs[0].shape[1]
    for k in range(NX):
        for m in range(NZ):
            first = pl.multiple_of((jnp.bitwise_xor(z, m) * NX + (x + k) % NX) * band, 16)
            out[pl.ds(first, band), :] = refs[2 * k + m // 2][m % 2]


def gather_from_owner(rep, own):
    band, columns = own.shape
    beside, across = swap_z(own, 1), swap_z(own, 2)
    others = [beside, across, swap_z(across, 1)]
    low, high = small_call(
        stack_kernel,
        [jax.ShapeDtypeStruct((2, band, columns), BF16)] * 2,
        "stack",
        [VMEM_SPEC] * NZ,
        own,
        *others,
    )
    low_minus, high_plus = shift_x(low, 1), shift_x(high, -1)
    high_minus, low_plus = shift_x(high, 1), shift_x(low, -1)
    low_cross, high_cross = shift_x(low_minus, 1), shift_x(high_plus, -1)
    tile = 384
    part = pl.BlockSpec((2, band, tile), lambda i: (0, 0, i))
    rows = NZ * NX * band
    return pl.pallas_call(
        assemble_kernel,
        grid=(columns // tile,),
        in_specs=[SMEM_SPEC] + [part] * 8,
        out_specs=pl.BlockSpec((rows, tile), lambda i: (0, i)),
        out_shape=jax.ShapeDtypeStruct((rows, columns), BF16),
        compiler_params=params(),
        cost_estimate=cost(1e3, 1e3),
        name="assemble",
    )(rep, low, high, low_plus, high_plus, low_cross, high_cross, low_minus, high_minus)


def exchange(rows, experts):
    slots, width = rows.shape
    block = rows.reshape(experts, slots // experts, width)
    return lax.all_to_all(block, "exp", split_axis=0, concat_axis=0, tiled=True).reshape(slots, width)


def per_device(w_in, w_out, mom_in, mom_out, frames, targets, routes, gates):
    experts = lax.axis_size("exp")
    replicas = lax.axis_size("rep")
    rep = lax.axis_index("rep")
    me = jnp.stack([rep, lax.axis_index("exp")]).astype(jnp.int32)
    capacity = 4 * frames.shape[2] // experts
    w_in, w_out, mom_in, mom_out = w_in[0], w_out[0], mom_in[0], mom_out[0]
    frames, targets, routes, gates = frames[0], targets[0], routes[0], gates[0]

    rows = lax.all_to_all(
        place_frames(routes[0], frames, experts, capacity),
        "exp",
        split_axis=0,
        concat_axis=0,
        tiled=True,
    )
    mine = jnp.zeros((8, frames.shape[1]), F32).at[:2].set(routes[1].T.astype(F32)), frames[1]
    mine = hold(mine, [rows])
    cross = [over_exp(array, flip_z=1) for array in mine]
    slope_one, active_one, produced = forward(rows, w_in, w_out, mine)
    (produced,) = hold([produced], cross)
    pieces = dispatch(capacity, me, *mine, *cross)
    returned = exchange(produced, experts)
    cot_one = exchange(place_residue(routes[0], gates[0], targets[0], returned, capacity, pieces), experts)
    active_t, one_t, rows_two, two_t = turned(me, active_one, rows, pieces)
    dh_one, theta_out, slope_two, active_two, produced = turn(
        one_t, rows_two, cot_one, w_in, w_out, slope_one, active_t
    )
    grad_one, part_one, active_t = ahead(w_out, active_t, cot_one, active_two)
    returned = exchange(produced, experts)
    cot_two = exchange(place_residue(routes[1], gates[1], targets[1], returned, capacity), experts)

    parts_out = change_out(me, replicas, grad_one, part_one, active_t, cot_two)
    far_out = start_far(parts_out)
    parts_in = change_in(
        me, replicas, one_t, two_t, w_in, dh_one, cot_two, theta_out, slope_two
    )
    near_out = near_sums(parts_out, far_out, parts_in[4:])
    terms_out, held = owner_terms(parts_out, far_out, near_out, parts_in[:2])
    parts_in = [*held, *parts_in[2:]]
    far_in = start_far(parts_in)
    terms_out = reduce_z(terms_out)
    near_in = near_sums(parts_in, far_in, parts_in[4:])
    terms_in = reduce_z(owner_terms(parts_in, far_in, near_in, [])[0])
    part_out, new_mom_out = outer_update(me, replicas, w_out, mom_out, terms_out)
    new_w_out = gather_from_owner(me, part_out)
    part_in, new_mom_in = outer_update(me, replicas, w_in, mom_in, terms_in)
    new_w_in = gather_from_owner(me, part_in)
    return (new_w_in[None], new_w_out[None], new_mom_in[None], new_mom_out[None])


def solution(mesh):
    in_specs = (
        P("exp", None, None),
        P("exp", None, None),
        P("exp", "rep", None),
        P("exp", "rep", None),
        P("rep", None, "exp", None),
        P("rep", None, "exp", None),
        P("rep", None, "exp", None),
        P("rep", None, "exp", None),
    )
    out_specs = (
        P("exp", None, None),
        P("exp", None, None),
        P("exp", "rep", None),
        P("exp", "rep", None),
    )
    return jax.shard_map(
        per_device, mesh=mesh, in_specs=in_specs, out_specs=out_specs, check_vma=False
    )
```

```python
import functools
import math

import jax
import jax.numpy as jnp
from jax import lax
from jax.experimental import pallas as pl
from jax.experimental.pallas import tpu as pltpu
from jax.sharding import PartitionSpec as P

F32 = jnp.float32
BF16 = jnp.bfloat16
MIB = 1 << 20
NX = 4
NZ = 4
NY = 4


SMEM_SPEC = pl.BlockSpec(memory_space=pltpu.SMEM)
VMEM_SPEC = pl.BlockSpec(memory_space=pltpu.VMEM)
ANY_SPEC = pl.BlockSpec(memory_space=pl.ANY)


def dot(left, right, on_left=1, on_right=0):
    return lax.dot_general(
        left, right, (((on_left,), (on_right,)), ((), ())), preferred_element_type=F32
    )


def slots_of(first, second):
    rows = first.shape[0]
    lane = lax.broadcasted_iota(jnp.int32, (rows, 128), 1)
    names_first, names_second = lane == first, lane == second
    named = jnp.where(names_first | names_second, 1.0, 0.0).astype(BF16)
    earlier = lax.broadcasted_iota(jnp.int32, (rows, rows), 0) > lax.broadcasted_iota(
        jnp.int32, (rows, rows), 1
    )
    count = dot(jnp.where(earlier, 1.0, 0.0).astype(BF16), named)
    slot_first = jnp.sum(jnp.where(names_first, count, 0.0), axis=1, keepdims=True)
    slot_second = jnp.sum(jnp.where(names_second, count, 0.0), axis=1, keepdims=True)
    return slot_first.astype(jnp.int32), slot_second.astype(jnp.int32)


def places(routes, capacity):
    first, second = routes[:, 0:1], routes[:, 1:2]
    slot_first, slot_second = slots_of(first, second)
    return first * capacity + slot_first, second * capacity + slot_second


def one_hot(place, size):
    lane = lax.broadcasted_iota(jnp.int32, (place.shape[0], size), 1)
    return jnp.where(lane == place, 1.0, 0.0).astype(BF16)


def gelu_and_slope(x):
    c = math.sqrt(2.0 / math.pi)
    square = x * x
    bent = jnp.tanh(c * (x + 0.044715 * (square * x)))
    half = 0.5 * (1.0 + bent)
    slope = half + 0.5 * x * (1.0 - bent * bent) * (c * (1.0 + 3 * 0.044715 * square))
    return x * half, slope


RATE, DECAY = 0.004, 0.1
KEEP = 1.0 - RATE * DECAY


def inverse(x):
    near = pl.reciprocal(x, approx=True)
    return near * (2.0 - x * near)


def after_one(weight, grad):
    return KEEP * weight - RATE * (grad * inverse(jnp.abs(grad) + 0.01))


def first_part(weight, grad_one):
    ratio = grad_one * inverse(jnp.abs(grad_one) + 0.01)
    return (1.0 - KEEP * KEEP) * weight + (RATE * KEEP) * ratio


def second_part(grad_one, grad_two):
    first = (0.09 / 0.19) * grad_one + (0.1 / 0.19) * grad_two
    second = (0.0475 / 0.0975) * (grad_one * grad_one) + (0.05 / 0.0975) * (grad_two * grad_two)
    return RATE * (first * inverse(second * lax.rsqrt(second + 1e-30) + 0.01))


def change_of_two(weight, grad_one, grad_two):
    first = (0.09 / 0.19) * grad_one + (0.1 / 0.19) * grad_two
    second = (0.0475 / 0.0975) * (grad_one * grad_one) + (0.05 / 0.0975) * (grad_two * grad_two)
    below_two = second * lax.rsqrt(second + 1e-30) + 0.01
    below_one = jnp.abs(grad_one) + 0.01
    over = KEEP * (grad_one * below_two) + first * below_one
    return (1.0 - KEEP * KEEP) * weight + RATE * (over * inverse(below_one * below_two))


def params(limit=48):
    return pltpu.CompilerParams(vmem_limit_bytes=limit * MIB)


def cost(flops, size):
    return pl.CostEstimate(flops=int(flops), bytes_accessed=int(size), transcendentals=0)


def small_call(kernel, out_shape, name, in_specs, *operands, **more):
    return pl.pallas_call(
        kernel,
        in_specs=in_specs,
        out_specs=jax.tree.map(lambda _: VMEM_SPEC, out_shape),
        out_shape=out_shape,
        compiler_params=params(),
        cost_estimate=cost(1e3, 1e3),
        name=name,
        **more,
    )(*operands)


def place_kernel(capacity, routes_ref, frames_ref, out_ref):
    experts, _, width = out_ref.shape
    size = experts * capacity
    first, second = places(routes_ref[...], capacity)
    spread = one_hot(first, size) + one_hot(second, size)
    placed = dot(spread, frames_ref[0], 0, 0).astype(BF16)
    out_ref[...] = placed.reshape(experts, capacity, width)


def place_frames(routes, frames, experts, capacity):
    return pl.pallas_call(
        functools.partial(place_kernel, capacity),
        grid=(1,),
        in_specs=[
            pl.BlockSpec(routes.shape, lambda i: (0, 0)),
            pl.BlockSpec((1, *frames.shape[1:]), lambda i: (0, 0, 0)),
        ],
        out_specs=pl.BlockSpec((experts, capacity, frames.shape[2]), lambda i: (0, 0, 0)),
        out_shape=jax.ShapeDtypeStruct((experts, capacity, frames.shape[2]), BF16),
        compiler_params=params(),
        cost_estimate=cost(2e9, 3e6),
        name="place_frames",
    )(routes, frames)


def spread_kernel(capacity, me_ref, routes_a, a_ref, routes_b, b_ref, *outs):
    me = me_ref[1]
    for block, (routes_ref, rows_ref) in enumerate(((routes_a, a_ref), (routes_b, b_ref))):
        routes = routes_ref[...].T.astype(jnp.int32)
        pair = routes[:, 0:1], routes[:, 1:2]
        hot = 0.0
        for expert, slot in zip(pair, slots_of(*pair)):
            ahead = jnp.bitwise_and((expert >> 2) - (me >> 2), NY - 1)
            here = jnp.bitwise_and(expert, 3) == jnp.bitwise_and(me, 3)
            hot += one_hot(jnp.where(here, ahead * capacity + slot, -1), NY * capacity)
        placed = dot(hot, rows_ref[...], 0, 0).astype(BF16)
        for ahead, out in enumerate(outs):
            out[block * capacity : (block + 1) * capacity, :] = placed[
                ahead * capacity : (ahead + 1) * capacity
            ]


def spread_rows(capacity, me, *blocks):
    width = blocks[1].shape[1]
    return small_call(
        functools.partial(spread_kernel, capacity),
        [jax.ShapeDtypeStruct((2 * capacity, width), BF16)] * NY,
        "spread_rows",
        [SMEM_SPEC] + [VMEM_SPEC] * 4,
        me,
        *blocks,
    )


def over_exp(array, along_y=0, flip_z=0, flip_core=0):
    pairs = []
    for y in range(NY):
        for z in range(2):
            for core in range(2):
                target = ((y + along_y) % NY, z ^ flip_z, core ^ flip_core)
                pairs.append((y * 4 + z * 2 + core, target[0] * 4 + target[1] * 2 + target[2]))
    return lax.ppermute(array, "exp", pairs)


def hold(arrays, after):
    return pl.pallas_call(
        lambda *refs: None,
        in_specs=[ANY_SPEC] * (len(arrays) + len(after)),
        out_specs=[ANY_SPEC] * len(arrays),
        out_shape=[jax.ShapeDtypeStruct(a.shape, a.dtype) for a in arrays],
        input_output_aliases={i: i for i in range(len(arrays))},
        cost_estimate=cost(1e3, 1e3),
        name="hold",
    )(*arrays, *after)


def dispatch(capacity, me, routes, own, cross_routes, cross):
    near = spread_rows(
        capacity, me, routes, own, over_exp(routes, flip_core=1), over_exp(own, flip_core=1)
    )
    far = spread_rows(
        capacity,
        me,
        cross_routes,
        cross,
        over_exp(cross_routes, flip_core=1),
        over_exp(cross, flip_core=1),
    )
    return [
        over_exp(piece, along_y=i) if i else piece for side in (near, far) for i, piece in enumerate(side)
    ]


def line_up(me, pieces, out):
    capacity = pieces[0].shape[0] // 2
    for at, piece in enumerate(pieces):
        for block in range(2):
            y = jnp.bitwise_and((me >> 2) - at % NY, NY - 1)
            place_of = jnp.bitwise_xor(jnp.bitwise_and(me, 3), 2 * (at // NY) + block)
            first = pl.multiple_of((y * 4 + place_of) * capacity, 32)
            out[pl.ds(first, capacity), :] = piece[block * capacity : (block + 1) * capacity, :]


def residue_kernel(capacity, routes_ref, gates_ref, targets_ref, returned_ref, *refs):
    out_ref = refs[-1]
    size = out_ref.shape[0]
    rows = routes_ref.shape[0]
    first, second = places(routes_ref[...], capacity)
    hot_first, hot_second = one_hot(first, size), one_hot(second, size)
    gate_first, gate_second = gates_ref[:, 0:1], gates_ref[:, 1:2]
    returned = returned_ref[...]
    combined = gate_first * dot(hot_first, returned) + gate_second * dot(hot_second, returned)
    residue = (combined - targets_ref[...].astype(F32)) * (1.0 / rows)
    cot_first = (gate_first * residue).astype(BF16)
    cot_second = (gate_second * residue).astype(BF16)
    out_ref[...] = (dot(hot_first, cot_first, 0, 0) + dot(hot_second, cot_second, 0, 0)).astype(BF16)


def place_residue(routes, gates, targets, returned, capacity, after=()):
    return small_call(
        functools.partial(residue_kernel, capacity),
        jax.ShapeDtypeStruct(returned.shape, BF16),
        "place_residue",
        [VMEM_SPEC] * 4 + [ANY_SPEC] * len(after),
        routes,
        gates,
        targets,
        returned,
        *after,
    )


def flat(ref):
    return ref[...].reshape(-1, ref.shape[-1])


def rows_spec(shape):
    return pl.BlockSpec(shape, lambda i: (0, 0, 0))


def forward_kernel(rows_ref, w_in_ref, w_out_ref, *refs):
    slope_ref, active_ref, produced_ref, total = refs[-4:]
    step = pl.program_id(0)
    active, slope_ref[...] = gelu_and_slope(dot(flat(rows_ref), w_in_ref[...]))
    active = active.astype(BF16)
    active_ref[...] = active
    part = dot(active, w_out_ref[...])

    @pl.when(step == 0)
    def _():
        total[...] = part

    @pl.when(step > 0)
    def _():
        total[...] += part

    @pl.when(step == pl.num_programs(0) - 1)
    def _():
        produced_ref[...] = total[...].astype(BF16)


def forward(rows, w_in, w_out, after, tile=512):
    experts, capacity, width = rows.shape
    slots = experts * capacity
    hid = w_in.shape[1]
    whole = pl.BlockSpec((slots, width), lambda i: (0, 0))
    by_col = pl.BlockSpec((slots, tile), lambda i: (0, i))
    return pl.pallas_call(
        forward_kernel,
        grid=(hid // tile,),
        in_specs=[
            rows_spec(rows.shape),
            pl.BlockSpec((width, tile), lambda i: (0, i)),
            pl.BlockSpec((tile, width), lambda i: (i, 0)),
        ]
        + [ANY_SPEC] * len(after),
        out_specs=[by_col, by_col, whole],
        out_shape=[
            jax.ShapeDtypeStruct((slots, hid), F32),
            jax.ShapeDtypeStruct((slots, hid), BF16),
            jax.ShapeDtypeStruct((slots, width), BF16),
        ],
        scratch_shapes=[pltpu.VMEM((slots, width), F32)],
        compiler_params=params(58),
        cost_estimate=cost(7e9, 1e7),
        name="forward",
    )(rows, w_in, w_out, *after)


def turned_kernel(me_ref, active_ref, rows_ref, *refs):
    pieces = refs[: 2 * NY]
    active_t_ref, rows_t_ref, next_ref, next_t_ref = refs[2 * NY :]
    active_t_ref[...] = active_ref[...].T

    @pl.when(pl.program_id(0) == 0)
    def _():
        rows_t_ref[...] = flat(rows_ref).T
        line_up(me_ref[1], pieces, next_ref)
        next_t_ref[...] = next_ref[...].T


def turned(me, active, rows, pieces, tile=512):
    slots, hid = active.shape
    width = rows.shape[2]
    piece = pl.BlockSpec(pieces[0].shape, lambda i: (0, 0))
    return pl.pallas_call(
        turned_kernel,
        grid=(hid // tile,),
        in_specs=[
            SMEM_SPEC,
            pl.BlockSpec((slots, tile), lambda i: (0, i)),
            rows_spec(rows.shape),
        ]
        + [piece] * len(pieces),
        out_specs=[
            pl.BlockSpec((tile, slots), lambda i: (i, 0)),
            pl.BlockSpec((width, slots), lambda i: (0, 0)),
            pl.BlockSpec((slots, width), lambda i: (0, 0)),
            pl.BlockSpec((width, slots), lambda i: (0, 0)),
        ],
        out_shape=[
            jax.ShapeDtypeStruct((hid, slots), BF16),
            jax.ShapeDtypeStruct((width, slots), BF16),
            jax.ShapeDtypeStruct((slots, width), BF16),
            jax.ShapeDtypeStruct((width, slots), BF16),
        ],
        compiler_params=params(58),
        cost_estimate=cost(5e9, 6e6),
        name="turned",
    )(me, active, rows, *pieces)


SUB = 256


def turn_kernel(
    turned_ref,
    next_ref,
    cot_ref,
    w_in_ref,
    w_out_ref,
    slope_ref,
    active_ref,
    dh_ref,
    theta_out_ref,
    slope_next_ref,
    active_next_ref,
    produced_ref,
    total,
):
    step = pl.program_id(0)

    cot = cot_ref[...]
    tile = w_in_ref.shape[1]
    part = 0.0
    for at in range(0, tile, SUB):
        cols = slice(at, at + SUB)
        w_out = w_out_ref[cols, :]
        dh = (dot(cot, w_out, 1, 1) * slope_ref[:, cols]).astype(BF16)
        dh_ref[:, cols] = dh
        grad_in = dot(turned_ref[...], dh)
        theta_in = after_one(w_in_ref[:, cols].astype(F32), grad_in).astype(BF16)
        grad_out = dot(active_ref[cols, :], cot)
        theta_out = after_one(w_out.astype(F32), grad_out).astype(BF16)
        theta_out_ref[cols, :] = theta_out
        active, slope_next_ref[:, cols] = gelu_and_slope(dot(next_ref[...], theta_in))
        active = active.astype(BF16)
        active_next_ref[:, cols] = active
        part += dot(active, theta_out)

    @pl.when(step == 0)
    def _():
        total[...] = part

    @pl.when(step > 0)
    def _():
        total[...] += part

    @pl.when(step == pl.num_programs(0) - 1)
    def _():
        produced_ref[...] = total[...].astype(BF16)


def turn(rows_t, next_rows, cot, w_in, w_out, slope, active_t, tile=512):
    slots, width = next_rows.shape
    hid = w_in.shape[1]
    whole = pl.BlockSpec((slots, width), lambda i: (0, 0))
    by_col = pl.BlockSpec((slots, tile), lambda i: (0, i))
    by_row = pl.BlockSpec((tile, width), lambda i: (i, 0))
    return pl.pallas_call(
        turn_kernel,
        grid=(hid // tile,),
        in_specs=[
            pl.BlockSpec((width, slots), lambda i: (0, 0)),
            whole,
            whole,
            pl.BlockSpec((width, tile), lambda i: (0, i)),
            by_row,
            by_col,
            pl.BlockSpec((tile, slots), lambda i: (i, 0)),
        ],
        out_specs=[by_col, by_row, by_col, by_col, whole],
        out_shape=[
            jax.ShapeDtypeStruct((slots, hid), BF16),
            jax.ShapeDtypeStruct((hid, width), BF16),
            jax.ShapeDtypeStruct((slots, hid), F32),
            jax.ShapeDtypeStruct((slots, hid), BF16),
            jax.ShapeDtypeStruct((slots, width), BF16),
        ],
        scratch_shapes=[pltpu.VMEM((slots, width), F32)],
        compiler_params=params(58),
        cost_estimate=cost(1.5e10, 2e7),
        name="turn",
    )(rows_t, next_rows, cot, w_in, w_out, slope, active_t)


PARTS = {
    0: (("own", 0), ("own", 2)),
    1: (("far_plus", 2), ("near_plus", 0)),
    2: (("far_minus", 0), ("far_plus", 0)),
    3: (("near_minus", 0), ("far_minus", 2)),
}
PART_SHARDS = {"far_minus": 4, "far_plus": 4, "near_minus": 2, "near_plus": 2, "own": 4}
HALVES = ((1, 3), (0, 2))


def store_band(k, m, change, outs):
    half = 0 if m in HALVES[0] else 1
    name, at = PARTS[k][half]
    outs[name][at + HALVES[half].index(m)] = change.astype(BF16)


def ahead_kernel(w_ref, active_t_ref, cot_ref, active_next_ref, grad_ref, part_ref, next_t_ref):
    grad = dot(active_t_ref[...], cot_ref[...])
    grad_ref[...] = grad
    part_ref[...] = first_part(w_ref[...].astype(F32), grad)
    next_t_ref[...] = active_next_ref[...].T


def ahead(w_out, active_t, cot, active_next, tile=384):
    hid, slots = active_t.shape
    width = cot.shape[1]
    by_row = pl.BlockSpec((tile, width), lambda i: (i, 0))
    by_slot = pl.BlockSpec((tile, slots), lambda i: (i, 0))
    return pl.pallas_call(
        ahead_kernel,
        grid=(hid // tile,),
        in_specs=[
            by_row,
            by_slot,
            pl.BlockSpec((slots, width), lambda i: (0, 0)),
            pl.BlockSpec((slots, tile), lambda i: (0, i)),
        ],
        out_specs=[by_row, by_row, by_slot],
        out_shape=[jax.ShapeDtypeStruct((hid, width), F32)] * 2
        + [jax.ShapeDtypeStruct((hid, slots), BF16)],
        compiler_params=params(58),
        cost_estimate=cost(7e9, 1.5e7),
        name="ahead",
    )(w_out, active_t, cot, active_next)


def change_out_kernel(rep_ref, grad_one, part_one, active_t, cot, *rest):
    outs = dict(zip(PART_SHARDS, rest[:5]))
    grad_two = rest[5]
    grad_two[...] = dot(active_t[...], cot[...])
    band = outs["own"].shape[1]
    x = rep_ref[0] % NX
    for m in range(NZ):

        @pl.when(pl.program_id(0) == m)
        def _():
            for k in range(NX):
                rows = pl.ds(pl.multiple_of((x + k) % NX * band, 16), band)
                change = part_one[rows, :] + second_part(grad_one[rows, :], grad_two[rows, :])
                store_band(k, m, change, outs)


def change_out(rep, replicas, grad_one, part_one, active_t, cot):
    hid, slots = active_t.shape
    width = cot.shape[1]
    band = hid // replicas
    tile = band * NX

    def z_of(i, rep_ref):
        return jnp.bitwise_xor(rep_ref[0] // NX, i)

    by_row = pl.BlockSpec((tile, width), lambda i, r: (z_of(i, r), 0))
    return pl.pallas_call(
        change_out_kernel,
        grid_spec=pltpu.PrefetchScalarGridSpec(
            num_scalar_prefetch=1,
            grid=(NZ,),
            in_specs=[
                by_row,
                by_row,
                pl.BlockSpec((tile, slots), lambda i, r: (z_of(i, r), 0)),
                pl.BlockSpec((slots, width), lambda i, r: (0, 0)),
            ],
            out_specs=[
                pl.BlockSpec((n, band, width), lambda i, r: (0, 0, 0)) for n in PART_SHARDS.values()
            ],
            scratch_shapes=[pltpu.VMEM((tile, width), F32)],
        ),
        out_shape=[jax.ShapeDtypeStruct((n, band, width), BF16) for n in PART_SHARDS.values()],
        compiler_params=params(),
        cost_estimate=cost(8e9, 1e7),
        name="change_out",
    )(rep, grad_one, part_one, active_t, cot)


def change_in_kernel(
    rep_ref, w_ref, one_t, dh_one, two_t, cot_two, theta_out, slope_two, *rest
):
    outs = dict(zip(PART_SHARDS, rest[:5]))
    grad_one, grad_two = rest[5:]
    upstream = dot(cot_two[...], theta_out[...], 1, 1)
    dh_two = (upstream * slope_two[...]).astype(BF16)
    grad_one[...] = dot(one_t[...], dh_one[...])
    grad_two[...] = dot(two_t[...], dh_two)
    band = outs["own"].shape[1]
    x, z = rep_ref[0] % NX, rep_ref[0] // NX
    for k in range(NX):
        for m in range(NZ):
            first = pl.multiple_of((jnp.bitwise_xor(z, m) * NX + (x + k) % NX) * band, 16)
            rows = pl.ds(first, band)
            change = change_of_two(w_ref[rows, :].astype(F32), grad_one[rows, :], grad_two[rows, :])
            store_band(k, m, change, outs)


def change_in(rep, replicas, one_t, two_t, w_in, dh_one, cot_two, theta_out, slope_two, tile=256):
    slots, hid = dh_one.shape
    width = one_t.shape[0]
    band = width // replicas
    whole = pl.BlockSpec((slots, width), lambda i: (0, 0))
    by_col = pl.BlockSpec((slots, tile), lambda i: (0, i))
    turned_spec = pl.BlockSpec((width, slots), lambda i: (0, 0))
    return pl.pallas_call(
        change_in_kernel,
        grid=(hid // tile,),
        in_specs=[
            SMEM_SPEC,
            pl.BlockSpec((width, tile), lambda i: (0, i)),
            turned_spec,
            by_col,
            turned_spec,
            whole,
            pl.BlockSpec((tile, width), lambda i: (i, 0)),
            by_col,
        ],
        out_specs=[pl.BlockSpec((n, band, tile), lambda i: (0, 0, i)) for n in PART_SHARDS.values()],
        out_shape=[jax.ShapeDtypeStruct((n, band, hid), BF16) for n in PART_SHARDS.values()],
        scratch_shapes=[
            pltpu.VMEM((width, tile), F32),
            pltpu.VMEM((width, tile), F32),
        ],
        compiler_params=params(48),
        cost_estimate=cost(1.2e10, 1.5e7),
        name="change_in",
    )(rep, w_in, one_t, dh_one, two_t, cot_two, theta_out, slope_two)


def rep_permutation(step_x, flip_z):
    pairs = []
    for z in range(NZ):
        for x in range(NX):
            pairs.append((z * NX + x, (z ^ flip_z) * NX + (x + step_x) % NX))
    return pairs


def shift_x(array, step):
    return lax.ppermute(array, "rep", rep_permutation(step, 0))


def swap_z(array, flip):
    return lax.ppermute(array, "rep", rep_permutation(0, flip))


def near_kernel(near_minus, near_plus, from_plus, from_minus, *refs):
    to_minus, to_plus = refs[-2:]
    to_minus[...] = (near_minus[...].astype(F32) + from_plus[:2].astype(F32)).astype(BF16)
    to_plus[...] = (near_plus[...].astype(F32) + from_minus[:2].astype(F32)).astype(BF16)


def sum_kernel(held, own, from_plus, from_minus, last_plus, last_minus, *refs):
    outs = refs[2 * held :]
    for half, members in enumerate(HALVES):
        for i, m in enumerate(members):
            total = own[2 * half + i].astype(F32)
            if half == 0:
                total += from_minus[2 + i].astype(F32) + last_plus[i].astype(F32)
            else:
                total += from_plus[2 + i].astype(F32) + last_minus[i].astype(F32)
            outs[m][...] = total.astype(outs[m].dtype)


def start_far(parts):
    return shift_x(parts[0], -1), shift_x(parts[1], 1)


def near_sums(parts, far, after):
    return small_call(
        near_kernel,
        [jax.ShapeDtypeStruct(parts[2].shape, BF16)] * 2,
        "near",
        [VMEM_SPEC] * 4 + [ANY_SPEC] * len(after),
        parts[2],
        parts[3],
        *far,
        *after,
    )


def owner_terms(parts, far, near, held):
    band_shape = parts[4].shape[1:]
    last = shift_x(near[0], -1), shift_x(near[1], 1)
    out = pl.pallas_call(
        functools.partial(sum_kernel, len(held)),
        in_specs=[VMEM_SPEC] * 5 + [ANY_SPEC] * len(held),
        out_specs=[ANY_SPEC] * len(held) + [VMEM_SPEC] * NZ,
        out_shape=[jax.ShapeDtypeStruct(a.shape, BF16) for a in held]
        + [jax.ShapeDtypeStruct(band_shape, F32 if m == 0 else BF16) for m in range(NZ)],
        input_output_aliases={5 + i: i for i in range(len(held))},
        compiler_params=params(),
        cost_estimate=cost(1e3, 1e3),
        name="sums",
    )(parts[4], *far, *last, *held)
    return out[len(held) :], out[: len(held)]


def middle_kernel(keep, other, across):
    across[...] = (keep[...].astype(F32) + other[...].astype(F32)).astype(BF16)


def reduce_z(terms):
    return [terms[0]] + [swap_z(terms[m], m) for m in range(1, NZ)]


def reduce_z_by_halves(terms):
    beside, third = swap_z(terms[1], 1), swap_z(terms[3], 1)
    across = small_call(
        middle_kernel,
        jax.ShapeDtypeStruct(third.shape, BF16),
        "middle",
        [VMEM_SPEC] * 2,
        terms[2],
        third,
    )
    return [terms[0], beside, swap_z(across, 2)]


def update_kernel(replicas, me_ref, w_ref, mom_ref, *refs):
    new_w, new_mom = refs[-2:]
    summed = refs[0][...]
    for term in refs[1:-2]:
        summed += term[...].astype(F32)
    averaged = summed * (1.0 / replicas)
    momentum = 0.9 * mom_ref[...] + averaged
    new_mom[...] = momentum
    new_w[...] = (w_ref[...].astype(F32) - 0.7 * (averaged + 0.9 * momentum)).astype(BF16)


def outer_update(rep, replicas, w, momentum, terms):
    band, columns = momentum.shape
    whole = pl.BlockSpec((band, columns), lambda i, r: (0, 0))
    return pl.pallas_call(
        functools.partial(update_kernel, replicas),
        grid_spec=pltpu.PrefetchScalarGridSpec(
            num_scalar_prefetch=1,
            grid=(1,),
            in_specs=[pl.BlockSpec((band, columns), lambda i, r: (r[0], 0))] + [whole] * (1 + len(terms)),
            out_specs=[whole] * 2,
        ),
        out_shape=[
            jax.ShapeDtypeStruct((band, columns), BF16),
            jax.ShapeDtypeStruct((band, columns), F32),
        ],
        compiler_params=params(),
        cost_estimate=cost(1e3, 1e3),
        name="update",
    )(rep, w, momentum, *terms)


def stack_kernel(one, two, three, four, low, high):
    low[0], low[1], high[0], high[1] = one[...], two[...], three[...], four[...]


def assemble_kernel(rep_ref, *refs):
    out = refs[-1]
    x, z = rep_ref[0] % NX, rep_ref[0] // NX
    band = refs[0].shape[1]
    for k in range(NX):
        for m in range(NZ):
            first = pl.multiple_of((jnp.bitwise_xor(z, m) * NX + (x + k) % NX) * band, 16)
            out[pl.ds(first, band), :] = refs[2 * k + m // 2][m % 2]


def gather_from_owner(rep, own):
    band, columns = own.shape
    beside, across = swap_z(own, 1), swap_z(own, 2)
    others = [beside, across, swap_z(across, 1)]
    low, high = small_call(
        stack_kernel,
        [jax.ShapeDtypeStruct((2, band, columns), BF16)] * 2,
        "stack",
        [VMEM_SPEC] * NZ,
        own,
        *others,
    )
    low_minus, high_plus = shift_x(low, 1), shift_x(high, -1)
    high_minus, low_plus = shift_x(high, 1), shift_x(low, -1)
    low_cross, high_cross = shift_x(low_minus, 1), shift_x(high_plus, -1)
    tile = 384
    part = pl.BlockSpec((2, band, tile), lambda i: (0, 0, i))
    rows = NZ * NX * band
    return pl.pallas_call(
        assemble_kernel,
        grid=(columns // tile,),
        in_specs=[SMEM_SPEC] + [part] * 8,
        out_specs=pl.BlockSpec((rows, tile), lambda i: (0, i)),
        out_shape=jax.ShapeDtypeStruct((rows, columns), BF16),
        compiler_params=params(),
        cost_estimate=cost(1e3, 1e3),
        name="assemble",
    )(rep, low, high, low_plus, high_plus, low_cross, high_cross, low_minus, high_minus)


def exchange(rows, experts):
    slots, width = rows.shape
    block = rows.reshape(experts, slots // experts, width)
    return lax.all_to_all(block, "exp", split_axis=0, concat_axis=0, tiled=True).reshape(slots, width)


def per_device(w_in, w_out, mom_in, mom_out, frames, targets, routes, gates):
    experts = lax.axis_size("exp")
    replicas = lax.axis_size("rep")
    rep = lax.axis_index("rep")
    me = jnp.stack([rep, lax.axis_index("exp")]).astype(jnp.int32)
    capacity = 4 * frames.shape[2] // experts
    w_in, w_out, mom_in, mom_out = w_in[0], w_out[0], mom_in[0], mom_out[0]
    frames, targets, routes, gates = frames[0], targets[0], routes[0], gates[0]

    rows = lax.all_to_all(
        place_frames(routes[0], frames, experts, capacity),
        "exp",
        split_axis=0,
        concat_axis=0,
        tiled=True,
    )
    mine = jnp.zeros((8, frames.shape[1]), F32).at[:2].set(routes[1].T.astype(F32)), frames[1]
    mine = hold(mine, [rows])
    cross = [over_exp(array, flip_z=1) for array in mine]
    slope_one, active_one, produced = forward(rows, w_in, w_out, mine)
    (produced,) = hold([produced], cross)
    pieces = dispatch(capacity, me, *mine, *cross)
    returned = exchange(produced, experts)
    cot_one = exchange(place_residue(routes[0], gates[0], targets[0], returned, capacity, pieces), experts)
    active_t, one_t, rows_two, two_t = turned(me, active_one, rows, pieces)
    dh_one, theta_out, slope_two, active_two, produced = turn(
        one_t, rows_two, cot_one, w_in, w_out, slope_one, active_t
    )
    grad_one, part_one, active_t = ahead(w_out, active_t, cot_one, active_two)
    returned = exchange(produced, experts)
    cot_two = exchange(place_residue(routes[1], gates[1], targets[1], returned, capacity), experts)

    parts_out = change_out(me, replicas, grad_one, part_one, active_t, cot_two)
    far_out = start_far(parts_out)
    parts_in = change_in(
        me, replicas, one_t, two_t, w_in, dh_one, cot_two, theta_out, slope_two
    )
    near_out = near_sums(parts_out, far_out, parts_in[4:])
    terms_out, held = owner_terms(parts_out, far_out, near_out, parts_in[:2])
    parts_in = [*held, *parts_in[2:]]
    far_in = start_far(parts_in)
    terms_out = reduce_z_by_halves(terms_out)
    near_in = near_sums(parts_in, far_in, parts_in[4:])
    terms_in = reduce_z(owner_terms(parts_in, far_in, near_in, [])[0])
    part_out, new_mom_out = outer_update(me, replicas, w_out, mom_out, terms_out)
    new_w_out = gather_from_owner(me, part_out)
    part_in, new_mom_in = outer_update(me, replicas, w_in, mom_in, terms_in)
    new_w_in = gather_from_owner(me, part_in)
    return (new_w_in[None], new_w_out[None], new_mom_in[None], new_mom_out[None])


def solution(mesh):
    in_specs = (
        P("exp", None, None),
        P("exp", None, None),
        P("exp", "rep", None),
        P("exp", "rep", None),
        P("rep", None, "exp", None),
        P("rep", None, "exp", None),
        P("rep", None, "exp", None),
        P("rep", None, "exp", None),
    )
    out_specs = (
        P("exp", None, None),
        P("exp", None, None),
        P("exp", "rep", None),
        P("exp", "rep", None),
    )
    return jax.shard_map(
        per_device, mesh=mesh, in_specs=in_specs, out_specs=out_specs, check_vma=False
    )
```
